32 devices in a mesh: group: 4 (over z), member: 8 (over y, x, core).
Axes of the slice: x: 2, y: 2, z: 4, core: 2. Of those that a mesh axis runs over, the one named last changes fastest.
Arguments:
- diag_tiles: bfloat16 [512, 4, 128, 128], P(('group', 'member')), may hold values from -0.21875 to 0.21875
- diag_cols: int32 [512, 4], P(('group', 'member')), may hold values from 0 to 15
- offd_tiles: bfloat16 [512, 2, 128, 128], P(('group', 'member')), may hold values from -0.21875 to 0.21875
- offd_cols: int32 [512, 2], P(('group', 'member')), may hold values from 0 to 7, as said below
- offd_count: int32 [512], P(('group', 'member')), may hold values from 0 to 2
- p_tiles: bfloat16 [512, 2, 128, 128], P(('group', 'member')), may hold values from -2 to 2
- p_cols: int32 [512, 2], P(('group', 'member')), may hold values from 0 to 31, as said below
- send_rows: int32 [32, 8, 1], P(('group', 'member')), may hold values from 0 to 15
- coarse_cols: int32 [32, 8], replicated, may hold values from 0 to 31, as said below
Outputs:
- coarse_tiles: float32 [32, 8, 128, 128], P(('group', 'member'))
The draws below stay inside these ranges and needn't reach their ends.
Inputs may be any that keep to these rules, and one draw needn't show every extreme that they name: `p_cols`: the 2 entries of fine block row f on group g and member m are distinct coarse rows h * 8 + m with h one of g, (g + 1) % 4, (g + 2) % 4. `offd_cols`: A remote tile of a fine block row on member m reads a row sent by member (m - 1) % 8, (m + 1) % 8 or (m + 4) % 8. `coarse_cols`: the 8 entries of coarse row h * 8 + m are distinct; they are that row itself and the rows ((h + 1) % 4) * 8 + m, ((h - 1) % 4) * 8 + m, ((h + 2) % 4) * 8 + m, then four rows h2 * 8 + m2 with h2 among h - 1, h, h + 1, h + 2 and m2 among m - 1, m + 1, m + 8 // 2 (both modulo their counts).
All inputs are finite; a program needn't handle non-finite values.
Results may differ from the reference program's by a relative error of at most 0.005.
Values may be sent and summed in bfloat16 or wider, within the bound.
A program may use at most 128 MiB of HBM per device.

```python
import jax
import jax.numpy as jnp
from jax import lax

TILE = 128
ROWS = 16
DIAG = 4
OFFD = 2
PTILES = 2
CTILES = 8
SEND = 1
MEMBERS = 8
FINE = 512
COARSE = 32
N_GROUP = 4
N_MEMBER = 8


def draw_offd_cols(key, part):
    fine = ROWS * N_GROUP * N_MEMBER
    member_idx = jnp.arange(fine) // ROWS % N_MEMBER
    pick = jax.random.randint(key, (fine, OFFD), 0, 3)
    steps = jnp.where(pick == 0, N_MEMBER - 1, jnp.where(pick == 1, 1, N_MEMBER // 2))
    sender = (member_idx[:, None] + steps) % N_MEMBER
    within = jax.random.randint(jax.random.fold_in(key, 3), (fine, OFFD), 0, SEND)
    return (sender * SEND + within).astype(jnp.int32)


def draw_p_cols(key, part):
    fine = ROWS * N_GROUP * N_MEMBER
    device_idx = jnp.arange(fine) // ROWS
    member_idx = device_idx % N_MEMBER
    group_idx = device_idx // N_MEMBER
    omit = jax.random.randint(key, (fine,), 0, 3)
    flip = jax.random.randint(jax.random.fold_in(key, 5), (fine,), 0, 2)
    first_kind = jnp.where(omit == 0, 1, 0)
    second_kind = jnp.where(omit == 2, 1, 2)
    lead = jnp.where(flip == 0, first_kind, second_kind)
    trail = jnp.where(flip == 0, second_kind, first_kind)

    def offset(kind):
        return jnp.where(kind == 0, 0, jnp.where(kind == 1, 1, N_GROUP // 2))
    col_one = (group_idx + offset(lead)) % N_GROUP * N_MEMBER + member_idx
    col_two = (group_idx + offset(trail)) % N_GROUP * N_MEMBER + member_idx
    return jnp.stack([col_one, col_two], axis=1).astype(jnp.int32)


def draw_coarse_cols(key, part):
    total = N_GROUP * N_MEMBER
    rows_idx = jnp.arange(total)
    group_idx = rows_idx // N_MEMBER
    member_idx = rows_idx % N_MEMBER
    own = [(group_idx + shift) % N_GROUP * N_MEMBER + member_idx for shift in [0, 1, N_GROUP - 1, N_GROUP // 2]]
    candidates = []
    for shift in [N_GROUP - 1, 0, 1, N_GROUP // 2]:
        for step in [N_MEMBER - 1, 1, N_MEMBER // 2]:
            candidates.append((group_idx + shift) % N_GROUP * N_MEMBER + (member_idx + step) % N_MEMBER)
    pool = jnp.stack(candidates, axis=1)
    scores = jax.random.randint(jax.random.fold_in(key, 7), (total, 12), 0, 1 << 20) * 12 + jnp.arange(12)[None, :]
    order = jnp.argsort(scores, axis=1, stable=True)[:, :4]
    chosen = jnp.take_along_axis(pool, order, axis=1)
    return jnp.concatenate([jnp.stack(own, axis=1), chosen], axis=1).astype(jnp.int32)


def touch_ends(entries, stream_key, least, high):
    spot = [jax.random.randint(jax.random.fold_in(stream_key, axis), (), 0, length) for axis, length in enumerate(entries.shape)]
    longest = entries.shape.index(max(entries.shape))
    beside = spot[:longest] + [(spot[longest] + 1) % entries.shape[longest]] + spot[longest + 1:]
    return entries.at[tuple(spot)].set(least).at[tuple(beside)].set(high)


def steps_of(stream_key, dims, shards, smallest, top_value):
    level, own = 1.0, jax.random.fold_in(stream_key, 6)
    for axis_at, shards_of in shards:
        draws = jnp.exp(jax.random.uniform(jax.random.fold_in(own, axis_at), (shards_of,), jnp.float32, smallest / len(shards), top_value / len(shards)))
        level = level * jnp.repeat(draws, dims[axis_at] // shards_of).reshape([-1 if axis == axis_at else 1 for axis in range(len(dims))])
    return level


def normal_values(key, dims, width, bound, shards=(), held_as=jnp.bfloat16):
    level = steps_of(key, dims, shards, -0.22, 0.18) if shards else 1.0
    array = jax.random.normal(key, dims, jnp.float32) * width * level
    return jnp.minimum(jnp.maximum(array, -bound), bound).astype(held_as)


def setup_inputs(seed: int = 0) -> dict:
    key_list = jax.random.split(jax.random.key(seed), 10)
    return {
        "diag_tiles": normal_values(key_list[0], (FINE, DIAG, TILE, TILE), (TILE * (DIAG + OFFD)) ** -0.5, 0.21875, ((0, 32),)),
        "diag_cols": touch_ends(jax.random.randint(key_list[1], (FINE, DIAG), 0, ROWS), jax.random.fold_in(key_list[1], 1), 0, ROWS - 1).astype(jnp.int32),
        "offd_tiles": normal_values(key_list[2], (FINE, OFFD, TILE, TILE), (TILE * (DIAG + OFFD)) ** -0.5, 0.21875, ((0, 32),)),
        "offd_cols": draw_offd_cols(jax.random.fold_in(key_list[9], 71), 0),
        "offd_count": touch_ends(jax.random.randint(key_list[4], (FINE,), 0, OFFD + 1), jax.random.fold_in(key_list[4], 1), 0, OFFD).astype(jnp.int32),
        "p_tiles": normal_values(key_list[5], (FINE, PTILES, TILE, TILE), 0.33, 2.0, ((0, 32),)),
        "p_cols": draw_p_cols(jax.random.fold_in(key_list[9], 71), 0),
        "send_rows": touch_ends(jax.random.randint(key_list[7], (COARSE, MEMBERS, SEND), 0, ROWS), jax.random.fold_in(key_list[7], 1), 0, ROWS - 1).astype(jnp.int32),
        "coarse_cols": draw_coarse_cols(jax.random.fold_in(key_list[9], 71), 0),
    }


def product_terms(a_tiles, p_rows, p_ids, targets, live):
    ap = jnp.einsum('rkab,rkqbc->rkqac', a_tiles.astype(jnp.float32), p_rows.astype(jnp.float32)).astype(jnp.bfloat16)
    match = p_ids[:, None, None, :, :] == targets[:, :, :, None, None]
    match = jnp.logical_and(match, live[:, None, None, :, None])
    return jnp.einsum('rpskq,rkqac->rpsac', match.astype(jnp.float32), ap.astype(jnp.float32))


def reference(diag_tiles, diag_cols, offd_tiles, offd_cols, offd_count, p_tiles, p_cols, send_rows, coarse_cols):
    members = N_MEMBER
    groups = N_GROUP

    def device(index):
        group_idx = index // members
        member_idx = index % members
        base = index * ROWS

        def local(x):
            return lax.dynamic_slice_in_dim(x, base, ROWS, 0)

        senders = (group_idx * members + jnp.arange(members)).astype(jnp.int32)
        picked = send_rows[senders][:, member_idx, :]
        remote = (senders[:, None] * ROWS + picked).reshape(-1).astype(jnp.int32)
        rows_diag = (base + local(diag_cols)).astype(jnp.int32)
        rows_offd = remote[local(offd_cols)]
        own_cols = local(p_cols)
        own_tiles = local(p_tiles)
        targets = coarse_cols[own_cols]
        full_live = jnp.ones((ROWS, DIAG), dtype=bool)
        counted = jnp.arange(OFFD)[None, :] < local(offd_count)[:, None]
        summed = product_terms(local(diag_tiles), p_tiles[rows_diag], p_cols[rows_diag], targets, full_live)
        summed = summed + product_terms(local(offd_tiles), p_tiles[rows_offd], p_cols[rows_offd], targets, counted)
        y_tiles = summed.astype(jnp.bfloat16)
        products = jnp.einsum('rpba,rpsbc->rpsac', own_tiles.astype(jnp.float32), y_tiles.astype(jnp.float32))
        route = (jnp.arange(groups)[:, None, None] == (own_cols // members)[None]).astype(jnp.float32)
        return jnp.einsum('grp,rpsac->gsac', route, products, precision=lax.Precision.HIGHEST).astype(jnp.bfloat16)

    partials = lax.map(device, jnp.arange(groups * members).astype(jnp.int32))

    def add_group(total, grp):
        block = lax.dynamic_slice_in_dim(partials, grp * members, members, 0)
        return total + block.astype(jnp.float32), None

    start = jnp.zeros((members, groups, CTILES, TILE, TILE), jnp.float32)
    total, _ = lax.scan(add_group, start, jnp.arange(groups).astype(jnp.int32))
    return jnp.transpose(total, (1, 0, 2, 3, 4)).reshape(groups * members, CTILES, TILE, TILE)
```

```python
import functools

import jax
import jax.numpy as jnp
from jax import lax
from jax.experimental import pallas as pl
from jax.experimental.pallas import tpu as pltpu
from jax.sharding import PartitionSpec as P

MESH = pl.DeviceIdType.MESH
CHUNKS = 4


def kernel(
    G,
    M,
    dcols,
    ocols,
    ocount,
    pcols,
    srows,
    ccols,
    p_hbm,
    d_hbm,
    o_hbm,
    out,
    p_v,
    d_v,
    o_v,
    pm,
    pmt,
    x,
    ar,
    sbuf,
    rbuf,
    tl,
    tt,
    gs,
    gr,
    p_sem,
    d_sem,
    o_sem,
    ms_sem,
    mr_sem,
    gs_sem,
    gr_sem,
):
    R, PT, T = p_v.shape[0], p_v.shape[1], p_v.shape[2]
    D, O = d_v.shape[1], o_v.shape[1]
    S = srows.shape[2]
    CT = ccols.shape[1]
    per = R // CHUNKS
    hoff = (0, 1, G // 2)
    moff = (M - 1, 1, M // 2)
    back = (1, 0, 2)
    coff = (0, 1, G - 1, G // 2)
    B = len(hoff)
    g = lax.axis_index("group")
    m = lax.axis_index("member")
    f32, bf16 = jnp.float32, jnp.bfloat16

    p_copy = pltpu.make_async_copy(p_hbm, p_v, p_sem)
    p_copy.start()
    for c in range(CHUNKS):
        rows = pl.ds(c * per, per)
        pltpu.make_async_copy(d_hbm.at[rows], d_v.at[rows], d_sem.at[c]).start()
    o_copy = pltpu.make_async_copy(o_hbm, o_v, o_sem)
    o_copy.start()

    barrier = pltpu.get_barrier_semaphore()
    peers = [(g, lax.rem(m + d, M)) for d in moff]
    peers += [(lax.rem(g + d, G), m) for d in (1, G - 1, G // 2)]
    for peer in peers:
        pl.semaphore_signal(barrier, inc=1, device_id=peer, device_id_type=MESH)

    own = [lax.rem(g + d, G) * M + m for d in hoff]

    p_copy.wait()
    for f in range(R):
        parts = []
        for b in range(B):
            block = jnp.zeros((T, T), bf16)
            for q in range(PT):
                block = jnp.where(pcols[f, q] == own[b], p_v[f, q], block)
            parts.append(block)
        row = jnp.concatenate(parts, axis=1)
        pm[f] = row
        pmt[:, f * T : (f + 1) * T] = row.T

    for i in range(3):
        to = lax.rem(m + moff[i], M)
        for s in range(S):
            sbuf[i, s] = pm[srows[0, to, s]]

    pl.semaphore_wait(barrier, len(peers))
    m_copies = []
    for i in range(3):
        copy = pltpu.make_async_remote_copy(
            src_ref=sbuf.at[i],
            dst_ref=rbuf.at[back[i]],
            send_sem=ms_sem.at[i],
            recv_sem=mr_sem.at[back[i]],
            device_id=(g, lax.rem(m + moff[i], M)),
            device_id_type=MESH,
        )
        copy.start()
        m_copies.append(copy)

    for c in range(CHUNKS):
        rows = pl.ds(c * per, per)
        pltpu.make_async_copy(d_hbm.at[rows], d_v.at[rows], d_sem.at[c]).wait()
        for f in range(c * per, (c + 1) * per):
            left = jnp.concatenate([d_v[f, k] for k in range(D)], axis=1)
            right = jnp.concatenate([pm[dcols[f, k]] for k in range(D)], axis=0)
            x[f * T : (f + 1) * T, :] = jnp.dot(
                left, right, preferred_element_type=f32
            ).astype(bf16)
    local = jnp.dot(pmt[...], x[...], preferred_element_type=f32)
    tl[...] = local[:T]

    sent = []
    for b in range(1, B):
        rel = [(hoff[b] + d) % G for d in coff]
        slots = [(s, hoff.index(r)) for s, r in enumerate(rel) if r in hoff]
        sent.append([s for s, _ in slots])
        for at, (_, b2) in enumerate(slots):
            gs[b - 1, at] = local[b * T : (b + 1) * T, b2 * T : (b2 + 1) * T].astype(bf16)

    def group_copy(b, part, lo, n):
        where = pl.ds(lo, n)
        return pltpu.make_async_remote_copy(
            src_ref=gs.at[b - 1, where],
            dst_ref=gr.at[b - 1, where],
            send_sem=gs_sem.at[b - 1, part],
            recv_sem=gr_sem.at[b - 1, part],
            device_id=(lax.rem(g + hoff[b], G), m),
            device_id_type=MESH,
        )

    g_copies = [[None, None] for _ in range(B)]
    for b in range(B - 1, 0, -1):
        g_copies[b][0] = group_copy(b, 0, 0, len(sent[b - 1]))
        g_copies[b][0].start()

    o_copy.wait()
    ids = [lax.rem(m + moff[i], M) * S + s for i in range(3) for s in range(S)]
    zero = jnp.zeros((T, T), bf16)
    for f in range(R):
        for r, ident in enumerate(ids):
            block = None
            for k in range(O):
                live = jnp.logical_and(ocols[f, k] == ident, ocount[f] > k)
                term = jnp.where(live, o_v[f, k], zero)
                block = term if block is None else block + term
            ar[f * T : (f + 1) * T, r * T : (r + 1) * T] = block
    mid = jnp.dot(pmt[...], ar[...], preferred_element_type=f32).astype(bf16)
    tt[3 * B] = jnp.zeros(tt.shape[1:], f32)
    for i in range(3):
        m_copies[back[i]].wait_recv()
        res = None
        for s in range(S):
            r = i * S + s
            term = jnp.dot(
                mid[:, r * T : (r + 1) * T], rbuf[i, s], preferred_element_type=f32
            )
            res = term if res is None else res + term
        for b2 in range(B):
            tt[i * B + b2] = res[:, b2 * T : (b2 + 1) * T]

    cand = [
        lax.rem(g + hoff[b2], G) * M + lax.rem(m + moff[i], M)
        for i in range(3)
        for b2 in range(B)
    ]

    def spot(b, s):
        col = ccols[own[b], s]
        at = jnp.int32(3 * B)
        for n, c in enumerate(cand):
            at = jnp.where(col == c, n, at)
        return at

    base = len(coff)
    for b in range(B - 1, 0, -1):
        lo = len(sent[b - 1])
        for s in range(base, CT):
            gs[b - 1, lo + s - base] = tt[spot(b, s), b * T : (b + 1) * T, :].astype(bf16)
        g_copies[b][1] = group_copy(b, 1, lo, CT - base)
        g_copies[b][1].start()

    for b in range(1, B):
        g_copies[b][0].wait_recv()
    rel = [d % G for d in coff]
    for s in range(base):
        total = None
        if rel[s] in hoff:
            b2 = hoff.index(rel[s])
            total = tl[:, b2 * T : (b2 + 1) * T]
        for b in range(1, B):
            if s in sent[b - 1]:
                term = gr[b - 1, sent[b - 1].index(s)].astype(f32)
                total = term if total is None else total + term
        out[0, s] = jnp.zeros((T, T), f32) if total is None else total
    for b in range(1, B):
        g_copies[b][1].wait_recv()
    for s in range(base, CT):
        total = tt[spot(0, s), :T, :]
        for b in range(1, B):
            total = total + gr[b - 1, len(sent[b - 1]) + s - base].astype(f32)
        out[0, s] = total

    for copy in m_copies:
        copy.wait_send()
    for b in range(1, B):
        for part in range(2):
            g_copies[b][part].wait_send()


def on_device(
    G,
    M,
    diag_tiles,
    diag_cols,
    offd_tiles,
    offd_cols,
    offd_count,
    p_tiles,
    p_cols,
    send_rows,
    coarse_cols,
):
    R, PT, T, _ = p_tiles.shape
    D, O = diag_tiles.shape[1], offd_tiles.shape[1]
    S = send_rows.shape[2]
    CT = coarse_cols.shape[1]
    B = 3
    bf16, f32 = jnp.bfloat16, jnp.float32
    smem = pl.BlockSpec(memory_space=pltpu.SMEM)
    hbm = pl.BlockSpec(memory_space=pl.ANY)
    return pl.pallas_call(
        functools.partial(kernel, G, M),
        out_shape=jax.ShapeDtypeStruct((1, CT, T, T), f32),
        in_specs=[smem] * 6 + [hbm] * 3,
        out_specs=pl.BlockSpec(memory_space=pltpu.VMEM),
        scratch_shapes=[
            pltpu.VMEM((R, PT, T, T), bf16),
            pltpu.VMEM((R, D, T, T), bf16),
            pltpu.VMEM((R, O, T, T), bf16),
            pltpu.VMEM((R, T, B * T), bf16),
            pltpu.VMEM((B * T, R * T), bf16),
            pltpu.VMEM((R * T, B * T), bf16),
            pltpu.VMEM((R * T, 3 * S * T), bf16),
            pltpu.VMEM((3, S, T, B * T), bf16),
            pltpu.VMEM((3, S, T, B * T), bf16),
            pltpu.VMEM((T, B * T), f32),
            pltpu.VMEM((3 * B + 1, B * T, T), f32),
            pltpu.VMEM((B - 1, CT, T, T), bf16),
            pltpu.VMEM((B - 1, CT, T, T), bf16),
            pltpu.SemaphoreType.DMA,
            pltpu.SemaphoreType.DMA((CHUNKS,)),
            pltpu.SemaphoreType.DMA,
            pltpu.SemaphoreType.DMA((3,)),
            pltpu.SemaphoreType.DMA((3,)),
            pltpu.SemaphoreType.DMA((B - 1, 2)),
            pltpu.SemaphoreType.DMA((B - 1, 2)),
        ],
        compiler_params=pltpu.CompilerParams(
            collective_id=0, has_side_effects=True, vmem_limit_bytes=63 * 1024 * 1024
        ),
    )(
        diag_cols,
        offd_cols,
        offd_count,
        p_cols,
        send_rows,
        coarse_cols,
        p_tiles,
        diag_tiles,
        offd_tiles,
    )


def solution(mesh):
    return jax.shard_map(
        functools.partial(on_device, mesh.shape["group"], mesh.shape["member"]),
        mesh=mesh,
        in_specs=(
            P(("group", "member"), None, None, None),
            P(("group", "member"), None),
            P(("group", "member"), None, None, None),
            P(("group", "member"), None),
            P(("group", "member")),
            P(("group", "member"), None, None, None),
            P(("group", "member"), None),
            P(("group", "member"), None, None),
            P(),
        ),
        out_specs=P(("group", "member"), None, None, None),
        check_vma=False,
    )
```

```python
import functools

import jax
import jax.numpy as jnp
from jax import lax
from jax.experimental import pallas as pl
from jax.experimental.pallas import tpu as pltpu
from jax.sharding import PartitionSpec as P

MESH = pl.DeviceIdType.MESH
CHUNKS = 4


def kernel(
    G,
    M,
    dcols,
    ocols,
    ocount,
    pcols,
    srows,
    ccols,
    p_hbm,
    d_hbm,
    o_hbm,
    kept,
    got,
    p_v,
    d_v,
    o_v,
    pm,
    pmt,
    x,
    ar,
    sbuf,
    rbuf,
    zeros,
    kept_v,
    tt,
    gs,
    p_sem,
    d_sem,
    o_sem,
    ms_sem,
    mr_sem,
    gs_sem,
    gr_sem,
    z_sem,
    k_sem,
):
    R, PT, T = p_v.shape[0], p_v.shape[1], p_v.shape[2]
    D, O = d_v.shape[1], o_v.shape[1]
    S = srows.shape[1]
    CT = ccols.shape[0]
    per = R // CHUNKS
    hoff = (0, 1, G // 2)
    moff = (M - 1, 1, M // 2)
    back = (1, 0, 2)
    coff = (0, 1, G - 1, G // 2)
    B = len(hoff)
    g = lax.axis_index("group")
    m = lax.axis_index("member")
    f32, bf16 = jnp.float32, jnp.bfloat16

    o_copy = pltpu.make_async_copy(o_hbm, o_v, o_sem)
    p_copy = pltpu.make_async_copy(p_hbm, p_v, p_sem)
    p_copy.start()
    for c in range(CHUNKS):
        rows = pl.ds(c * per, per)
        pltpu.make_async_copy(d_hbm.at[rows], d_v.at[rows], d_sem.at[c]).start()
    o_copy.start()

    barrier = pltpu.get_barrier_semaphore()
    peers = [(g, lax.rem(m + d, M)) for d in moff]
    peers += [(lax.rem(g + d, G), m) for d in (1, G - 1, G // 2)]
    for peer in peers:
        pl.semaphore_signal(barrier, inc=1, device_id=peer, device_id_type=MESH)

    own = [lax.rem(g + d, G) * M + m for d in hoff]
    base = len(coff)

    sent = []
    for b in range(B):
        rel = [(hoff[b] + d) % G for d in coff]
        sent.append({s: hoff.index(r) for s, r in enumerate(rel) if r in hoff})
    zeros[...] = jnp.zeros((T, T), bf16)
    fills = [
        pltpu.make_async_copy(zeros, got.at[b - 1, s], z_sem.at[b - 1, s])
        for b in range(1, B)
        for s in range(base)
        if s not in sent[b]
    ]
    for fill in fills:
        fill.start()

    p_copy.wait()
    for f in range(R):
        parts = []
        for b in range(B):
            block = jnp.zeros((T, T), bf16)
            for q in range(PT):
                block = jnp.where(pcols[q, f] == own[b], p_v[f, q], block)
            parts.append(block)
        pm[f] = jnp.concatenate(parts, axis=1)

    for i in range(3):
        to = lax.rem(m + moff[i], M)
        for s in range(S):
            sbuf[i, s] = pm[srows[0, s, to]]

    pl.semaphore_wait(barrier, len(peers))
    m_copies = []
    for i in range(3):
        copy = pltpu.make_async_remote_copy(
            src_ref=sbuf.at[i],
            dst_ref=rbuf.at[back[i]],
            send_sem=ms_sem.at[i],
            recv_sem=mr_sem.at[back[i]],
            device_id=(g, lax.rem(m + moff[i], M)),
            device_id_type=MESH,
        )
        copy.start()
        m_copies.append(copy)

    ids = [lax.rem(m + moff[i], M) * S + s for i in range(3) for s in range(S)]
    zero = jnp.zeros((T, T), bf16)
    for c in range(CHUNKS):
        rows = pl.ds(c * per, per)
        pltpu.make_async_copy(d_hbm.at[rows], d_v.at[rows], d_sem.at[c]).wait()
        if c == CHUNKS - 1:
            o_copy.wait()
        for f in range(c * per, (c + 1) * per):
            left = jnp.concatenate([d_v[f, k] for k in range(D)], axis=1)
            right = jnp.concatenate([pm[dcols[k, f]] for k in range(D)], axis=0)
            x[f * T : (f + 1) * T, :] = jnp.dot(
                left, right, preferred_element_type=f32
            ).astype(bf16)
            pmt[:, f * T : (f + 1) * T] = pm[f].T
    local = jnp.dot(pmt[T:, :], x[...], preferred_element_type=f32)

    def group_copy(b, lo, n):
        where = pl.ds(lo, n)
        return pltpu.make_async_remote_copy(
            src_ref=gs.at[b - 1, where],
            dst_ref=got.at[b - 1, where],
            send_sem=gs_sem.at[b - 1, lo],
            recv_sem=gr_sem.at[b - 1, lo],
            device_id=(lax.rem(g + hoff[b], G), m),
            device_id_type=MESH,
        )

    g_copies = []
    for b in range(B - 1, 0, -1):
        for s, b2 in sent[b].items():
            gs[b - 1, s] = local[(b - 1) * T : b * T, b2 * T : (b2 + 1) * T].astype(bf16)
        lo = 0
        while lo < base:
            n = 0
            while lo + n < base and lo + n in sent[b]:
                n += 1
            if n:
                g_copies.append(group_copy(b, lo, n))
                g_copies[-1].start()
            lo += n + 1

    for f in range(R):
        for r, ident in enumerate(ids):
            block = None
            for k in range(O):
                live = jnp.logical_and(ocols[k, f] == ident, ocount[f] > k)
                term = jnp.where(live, o_v[f, k], zero)
                block = term if block is None else block + term
            ar[f * T : (f + 1) * T, r * T : (r + 1) * T] = block
    tt[3 * B] = jnp.zeros(tt.shape[1:], f32)

    def remote(lo, hi, arrive):
        mid = jnp.dot(pmt[lo:hi, :], ar[...], preferred_element_type=f32).astype(bf16)
        for i in range(3):
            if arrive:
                m_copies[back[i]].wait_recv()
            res = None
            for s in range(S):
                r = i * S + s
                term = jnp.dot(
                    mid[:, r * T : (r + 1) * T], rbuf[i, s], preferred_element_type=f32
                )
                res = term if res is None else res + term
            for b2 in range(B):
                tt[i * B + b2, lo:hi] = res[:, b2 * T : (b2 + 1) * T]

    cand = [
        lax.rem(g + hoff[b2], G) * M + lax.rem(m + moff[i], M)
        for i in range(3)
        for b2 in range(B)
    ]

    def spot(b, s):
        col = ccols[s, own[b]]
        at = jnp.int32(3 * B)
        for n, c in enumerate(cand):
            at = jnp.where(col == c, n, at)
        return at

    remote(T, B * T, True)
    for b in range(B - 1, 0, -1):
        for s in range(base, CT):
            gs[b - 1, s] = tt[spot(b, s), b * T : (b + 1) * T, :].astype(bf16)
        g_copies.append(group_copy(b, base, CT - base))
        g_copies[-1].start()

    local = jnp.dot(pmt[:T, :], x[...], preferred_element_type=f32)
    for s in range(base):
        if s in sent[0]:
            b2 = sent[0][s]
            kept_v[s] = local[:, b2 * T : (b2 + 1) * T]
        else:
            kept_v[s] = jnp.zeros((T, T), f32)
    remote(0, T, False)
    for s in range(base, CT):
        kept_v[s] = tt[spot(0, s), :T, :]
    keep = pltpu.make_async_copy(kept_v, kept, k_sem)
    keep.start()

    for fill in fills:
        fill.wait()
    keep.wait()
    for copy in m_copies:
        copy.wait_send()
    for copy in g_copies:
        copy.wait()


def on_device(
    G,
    M,
    diag_tiles,
    diag_cols,
    offd_tiles,
    offd_cols,
    offd_count,
    p_tiles,
    p_cols,
    send_rows,
    coarse_cols,
):
    R, PT, T, _ = p_tiles.shape
    D, O = diag_tiles.shape[1], offd_tiles.shape[1]
    S = send_rows.shape[2]
    CT = coarse_cols.shape[1]
    B = 3
    bf16, f32 = jnp.bfloat16, jnp.float32
    smem = pl.BlockSpec(memory_space=pltpu.SMEM)
    hbm = pl.BlockSpec(memory_space=pl.ANY)
    kept, got = pl.pallas_call(
        functools.partial(kernel, G, M),
        out_shape=(
            jax.ShapeDtypeStruct((CT, T, T), f32),
            jax.ShapeDtypeStruct((B - 1, CT, T, T), bf16),
        ),
        in_specs=[smem] * 6 + [hbm] * 3,
        out_specs=(hbm, hbm),
        scratch_shapes=[
            pltpu.VMEM((R, PT, T, T), bf16),
            pltpu.VMEM((R, D, T, T), bf16),
            pltpu.VMEM((R, O, T, T), bf16),
            pltpu.VMEM((R, T, B * T), bf16),
            pltpu.VMEM((B * T, R * T), bf16),
            pltpu.VMEM((R * T, B * T), bf16),
            pltpu.VMEM((R * T, 3 * S * T), bf16),
            pltpu.VMEM((3, S, T, B * T), bf16),
            pltpu.VMEM((3, S, T, B * T), bf16),
            pltpu.VMEM((T, T), bf16),
            pltpu.VMEM((CT, T, T), f32),
            pltpu.VMEM((3 * B + 1, B * T, T), f32),
            pltpu.VMEM((B - 1, CT, T, T), bf16),
            pltpu.SemaphoreType.DMA,
            pltpu.SemaphoreType.DMA((CHUNKS,)),
            pltpu.SemaphoreType.DMA,
            pltpu.SemaphoreType.DMA((3,)),
            pltpu.SemaphoreType.DMA((3,)),
            pltpu.SemaphoreType.DMA((B - 1, CT)),
            pltpu.SemaphoreType.DMA((B - 1, CT)),
            pltpu.SemaphoreType.DMA((B - 1, CT)),
            pltpu.SemaphoreType.DMA,
        ],
        compiler_params=pltpu.CompilerParams(
            collective_id=0, has_side_effects=True, vmem_limit_bytes=63 * 1024 * 1024
        ),
    )(
        diag_cols.T,
        offd_cols.T,
        offd_count,
        p_cols.T,
        jnp.swapaxes(send_rows, 1, 2),
        coarse_cols.T,
        p_tiles,
        diag_tiles,
        offd_tiles,
    )
    return (kept + got[0].astype(f32) + got[1].astype(f32))[None]


def solution(mesh):
    return jax.shard_map(
        functools.partial(on_device, mesh.shape["group"], mesh.shape["member"]),
        mesh=mesh,
        in_specs=(
            P(("group", "member"), None, None, None),
            P(("group", "member"), None),
            P(("group", "member"), None, None, None),
            P(("group", "member"), None),
            P(("group", "member")),
            P(("group", "member"), None, None, None),
            P(("group", "member"), None),
            P(("group", "member"), None, None),
            P(),
        ),
        out_specs=P(("group", "member"), None, None, None),
        check_vma=False,
    )
```

```python
import functools

import jax
import jax.numpy as jnp
from jax import lax
from jax.experimental import pallas as pl
from jax.experimental.pallas import tpu as pltpu
from jax.sharding import PartitionSpec as P

MESH = pl.DeviceIdType.MESH
CHUNKS = 4


def kernel(
    G,
    M,
    dcols,
    ocols,
    ocount,
    pcols,
    srows,
    ccols,
    p_hbm,
    d_hbm,
    o_hbm,
    kept,
    got,
    p_v,
    d_v,
    o_v,
    pm,
    pmt,
    x,
    ar,
    sbuf,
    rbuf,
    zeros,
    kept_v,
    tt,
    gs,
    loc,
    fed_v,
    p_sem,
    d_sem,
    o_sem,
    ms_sem,
    mr_sem,
    gs_sem,
    gr_sem,
    z_sem,
    k_sem,
    f_sem,
):
    R, PT, T = p_v.shape[0], p_v.shape[1], p_v.shape[2]
    D, O = d_v.shape[1], o_v.shape[1]
    S = srows.shape[1]
    CT = ccols.shape[0]
    per = R // CHUNKS
    hoff = (0, 1, G // 2)
    moff = (M - 1, 1, M // 2)
    back = (1, 0, 2)
    coff = (0, 1, G - 1, G // 2)
    B = len(hoff)
    g = lax.axis_index("group")
    m = lax.axis_index("member")
    f32, bf16 = jnp.float32, jnp.bfloat16

    o_copy = pltpu.make_async_copy(o_hbm, o_v, o_sem)
    p_copy = pltpu.make_async_copy(p_hbm, p_v, p_sem)
    p_copy.start()
    for c in range(CHUNKS):
        rows = pl.ds(c * per, per)
        pltpu.make_async_copy(d_hbm.at[rows], d_v.at[rows], d_sem.at[c]).start()
    o_copy.start()

    barrier = pltpu.get_barrier_semaphore()
    peers = [(g, lax.rem(m + d, M)) for d in moff]
    peers += [(lax.rem(g + d, G), m) for d in (1, G - 1, G // 2)]
    for peer in peers:
        pl.semaphore_signal(barrier, inc=1, device_id=peer, device_id_type=MESH)

    own = [lax.rem(g + d, G) * M + m for d in hoff]
    base = len(coff)

    sent = []
    for b in range(B):
        rel = [(hoff[b] + d) % G for d in coff]
        sent.append({s: hoff.index(r) for s, r in enumerate(rel) if r in hoff})
    relays = {1: 1, 2: 2} if G == 4 else {}
    feeds = {1: 3, 2: 0} if G == 4 else {}

    def runs(have):
        found = []
        for s in sorted(have):
            if found and sum(found[-1]) == s:
                found[-1] = (found[-1][0], found[-1][1] + 1)
            else:
                found.append((s, 1))
        return found

    def fill(b, lo, n):
        where = pl.ds(lo, n)
        return pltpu.make_async_copy(zeros.at[pl.ds(0, n)], got.at[b - 1, where], z_sem.at[b - 1, lo])

    def each_fill(act):
        for b in range(1, B):
            gap = runs(set(range(base)) - set(sent[b]))

            def some(b=b, gap=gap):
                for lo, n in gap:
                    act(fill(b, lo, n))

            if not relays:
                some()
                continue
            fed = (relays[b] + hoff[b]) % G
            other = B - b
            pl.when(jnp.logical_and(g != (relays[other] + hoff[other]) % G, g != fed))(some)

            @pl.when(g == fed)
            def _(other=other):
                act(fill(other, 0, CT))

    zeros[...] = jnp.zeros((CT, T, T), bf16)
    each_fill(lambda copy: copy.start())

    p_copy.wait()
    for f in range(R):
        parts = []
        for b in range(B):
            block = jnp.zeros((T, T), bf16)
            for q in range(PT):
                block = jnp.where(pcols[q, f] == own[b], p_v[f, q], block)
            parts.append(block)
        pm[f] = jnp.concatenate(parts, axis=1)

    for i in range(3):
        to = lax.rem(m + moff[i], M)
        for s in range(S):
            sbuf[i, s] = pm[srows[0, s, to]]

    pl.semaphore_wait(barrier, len(peers))
    m_copies = []
    for i in range(3):
        copy = pltpu.make_async_remote_copy(
            src_ref=sbuf.at[i],
            dst_ref=rbuf.at[back[i]],
            send_sem=ms_sem.at[i],
            recv_sem=mr_sem.at[back[i]],
            device_id=(g, lax.rem(m + moff[i], M)),
            device_id_type=MESH,
        )
        copy.start()
        m_copies.append(copy)

    ids = [lax.rem(m + moff[i], M) * S + s for i in range(3) for s in range(S)]
    zero = jnp.zeros((T, T), bf16)
    for c in range(CHUNKS):
        rows = pl.ds(c * per, per)
        pltpu.make_async_copy(d_hbm.at[rows], d_v.at[rows], d_sem.at[c]).wait()
        if c == CHUNKS - 1:
            o_copy.wait()
        for f in range(c * per, (c + 1) * per):
            left = jnp.concatenate([d_v[f, k] for k in range(D)], axis=1)
            right = jnp.concatenate([pm[dcols[k, f]] for k in range(D)], axis=0)
            x[f * T : (f + 1) * T, :] = jnp.dot(
                left, right, preferred_element_type=f32
            ).astype(bf16)
            pmt[:, f * T : (f + 1) * T] = pm[f].T
    local = jnp.dot(pmt[T:, :], x[...], preferred_element_type=f32)

    def group_copy(b, lo, n):
        where = pl.ds(lo, n)
        return pltpu.make_async_remote_copy(
            src_ref=gs.at[b - 1, where],
            dst_ref=got.at[b - 1, where],
            send_sem=gs_sem.at[b - 1, lo],
            recv_sem=gr_sem.at[b - 1, lo],
            device_id=(lax.rem(g + hoff[b], G), m),
            device_id_type=MESH,
        )

    def feed_copy(b, lo, n):
        where = pl.ds(lo, n)
        return pltpu.make_async_remote_copy(
            src_ref=gs.at[b - 1, where],
            dst_ref=fed_v.at[where],
            send_sem=gs_sem.at[b - 1, lo],
            recv_sem=f_sem.at[lo],
            device_id=(relays[B - b], m),
            device_id_type=MESH,
        )

    last = [(base, CT - base)]

    def each_send(b, spans, act):
        def direct():
            for lo, n in spans:
                act(group_copy(b, lo, n))

        if not relays:
            direct()
            return
        pl.when(jnp.logical_and(g != feeds[b], g != relays[b]))(direct)

        @pl.when(g == feeds[b])
        def _():
            for lo, n in spans:
                act(feed_copy(b, lo, n))

    def each_relay(first, act):
        for b in relays:
            pl.when(g == relays[b])(functools.partial(act, b, first))

    def add_and_send(b, first):
        spans = runs(sent[B - b]) if first else last
        for lo, n in spans:
            feed_copy(B - b, lo, n).wait_recv()
        lo, n = (0, base) if first else last[0]
        come = [s for at, count in spans for s in range(at, at + count)]
        for s in range(lo, lo + n):
            total = None
            if not first:
                total = tt[spot(b, s), b * T : (b + 1) * T, :]
            elif s in sent[b]:
                b2 = sent[b][s]
                total = loc[(b - 1) * T : b * T, b2 * T : (b2 + 1) * T]
            if s in come:
                term = fed_v[s].astype(f32)
                total = term if total is None else total + term
            gs[b - 1, s] = total.astype(bf16)
        group_copy(b, lo, n).start()

    if relays:
        loc[...] = local
    for b in range(B - 1, 0, -1):
        for s, b2 in sent[b].items():
            gs[b - 1, s] = local[(b - 1) * T : b * T, b2 * T : (b2 + 1) * T].astype(bf16)
        each_send(b, runs(sent[b]), lambda copy: copy.start())

    for f in range(R):
        for r, ident in enumerate(ids):
            block = None
            for k in range(O):
                live = jnp.logical_and(ocols[k, f] == ident, ocount[f] > k)
                term = jnp.where(live, o_v[f, k], zero)
                block = term if block is None else block + term
            ar[f * T : (f + 1) * T, r * T : (r + 1) * T] = block
    tt[3 * B] = jnp.zeros(tt.shape[1:], f32)

    def remote(lo, hi, arrive):
        mid = jnp.dot(pmt[lo:hi, :], ar[...], preferred_element_type=f32).astype(bf16)
        for i in range(3):
            if arrive:
                m_copies[back[i]].wait_recv()
            res = None
            for s in range(S):
                r = i * S + s
                term = jnp.dot(
                    mid[:, r * T : (r + 1) * T], rbuf[i, s], preferred_element_type=f32
                )
                res = term if res is None else res + term
            for b2 in range(B):
                tt[i * B + b2, lo:hi] = res[:, b2 * T : (b2 + 1) * T]

    cand = [
        lax.rem(g + hoff[b2], G) * M + lax.rem(m + moff[i], M)
        for i in range(3)
        for b2 in range(B)
    ]

    def spot(b, s):
        col = ccols[s, own[b]]
        at = jnp.int32(3 * B)
        for n, c in enumerate(cand):
            at = jnp.where(col == c, n, at)
        return at

    remote(T, B * T, True)
    for b in range(B - 1, 0, -1):
        for s in range(base, CT):
            gs[b - 1, s] = tt[spot(b, s), b * T : (b + 1) * T, :].astype(bf16)
        each_send(b, last, lambda copy: copy.start())
    each_relay(True, add_and_send)

    local = jnp.dot(pmt[:T, :], x[...], preferred_element_type=f32)
    for s in range(base):
        if s in sent[0]:
            b2 = sent[0][s]
            kept_v[s] = local[:, b2 * T : (b2 + 1) * T]
        else:
            kept_v[s] = jnp.zeros((T, T), f32)
    remote(0, T, False)
    for s in range(base, CT):
        kept_v[s] = tt[spot(0, s), :T, :]
    keep = pltpu.make_async_copy(kept_v, kept, k_sem)
    keep.start()

    each_relay(False, add_and_send)

    each_fill(lambda copy: copy.wait())
    keep.wait()
    for copy in m_copies:
        copy.wait_send()
    for b in range(1, B):
        each_send(b, runs(sent[b]) + last, lambda copy: copy.wait_send())
        if not relays:
            for lo, n in runs(sent[b]) + last:
                group_copy(b, lo, n).wait_recv()
            continue
        whole = [(0, base)] + last

        @pl.when(g == relays[b])
        def _(b=b):
            for lo, n in whole:
                group_copy(b, lo, n).wait_send()

        fed = (relays[b] + hoff[b]) % G

        @pl.when(g == fed)
        def _(b=b):
            for lo, n in whole:
                group_copy(b, lo, n).wait_recv()

        @pl.when(lax.rem(g, 2) == 1)
        def _(b=b):
            for lo, n in runs(sent[b]) + last:
                group_copy(b, lo, n).wait_recv()


def on_device(
    G,
    M,
    diag_tiles,
    diag_cols,
    offd_tiles,
    offd_cols,
    offd_count,
    p_tiles,
    p_cols,
    send_rows,
    coarse_cols,
):
    R, PT, T, _ = p_tiles.shape
    D, O = diag_tiles.shape[1], offd_tiles.shape[1]
    S = send_rows.shape[2]
    CT = coarse_cols.shape[1]
    B = 3
    bf16, f32 = jnp.bfloat16, jnp.float32
    smem = pl.BlockSpec(memory_space=pltpu.SMEM)
    hbm = pl.BlockSpec(memory_space=pl.ANY)
    kept, got = pl.pallas_call(
        functools.partial(kernel, G, M),
        out_shape=(
            jax.ShapeDtypeStruct((CT, T, T), f32),
            jax.ShapeDtypeStruct((B - 1, CT, T, T), bf16),
        ),
        in_specs=[smem] * 6 + [hbm] * 3,
        out_specs=(hbm, hbm),
        scratch_shapes=[
            pltpu.VMEM((R, PT, T, T), bf16),
            pltpu.VMEM((R, D, T, T), bf16),
            pltpu.VMEM((R, O, T, T), bf16),
            pltpu.VMEM((R, T, B * T), bf16),
            pltpu.VMEM((B * T, R * T), bf16),
            pltpu.VMEM((R * T, B * T), bf16),
            pltpu.VMEM((R * T, 3 * S * T), bf16),
            pltpu.VMEM((3, S, T, B * T), bf16),
            pltpu.VMEM((3, S, T, B * T), bf16),
            pltpu.VMEM((CT, T, T), bf16),
            pltpu.VMEM((CT, T, T), f32),
            pltpu.VMEM((3 * B + 1, B * T, T), f32),
            pltpu.VMEM((B - 1, CT, T, T), bf16),
            pltpu.VMEM(((B - 1) * T, B * T), f32),
            pltpu.VMEM((CT, T, T), bf16),
            pltpu.SemaphoreType.DMA,
            pltpu.SemaphoreType.DMA((CHUNKS,)),
            pltpu.SemaphoreType.DMA,
            pltpu.SemaphoreType.DMA((3,)),
            pltpu.SemaphoreType.DMA((3,)),
            pltpu.SemaphoreType.DMA((B - 1, CT)),
            pltpu.SemaphoreType.DMA((B - 1, CT)),
            pltpu.SemaphoreType.DMA((B - 1, CT)),
            pltpu.SemaphoreType.DMA,
            pltpu.SemaphoreType.DMA((CT,)),
        ],
        compiler_params=pltpu.CompilerParams(
            collective_id=0, has_side_effects=True, vmem_limit_bytes=63 * 1024 * 1024
        ),
    )(
        diag_cols.T,
        offd_cols.T,
        offd_count,
        p_cols.T,
        jnp.swapaxes(send_rows, 1, 2),
        coarse_cols.T,
        p_tiles,
        diag_tiles,
        offd_tiles,
    )
    return (kept + got[0].astype(f32) + got[1].astype(f32))[None]


def solution(mesh):
    return jax.shard_map(
        functools.partial(on_device, mesh.shape["group"], mesh.shape["member"]),
        mesh=mesh,
        in_specs=(
            P(("group", "member"), None, None, None),
            P(("group", "member"), None),
            P(("group", "member"), None, None, None),
            P(("group", "member"), None),
            P(("group", "member")),
            P(("group", "member"), None, None, None),
            P(("group", "member"), None),
            P(("group", "member"), None, None),
            P(),
        ),
        out_specs=P(("group", "member"), None, None, None),
        check_vma=False,
    )
```

```python
import functools

import jax
import jax.numpy as jnp
from jax import lax
from jax.experimental import pallas as pl
from jax.experimental.pallas import tpu as pltpu
from jax.sharding import PartitionSpec as P

MESH = pl.DeviceIdType.MESH
CHUNKS = 4


def kernel(
    G,
    M,
    dcols,
    ocols,
    ocount,
    pcols,
    srows,
    ccols,
    p_hbm,
    d_hbm,
    o_hbm,
    kept,
    got,
    p_v,
    d_v,
    o_v,
    pm,
    pmt,
    x,
    ar,
    sbuf,
    rbuf,
    zeros,
    kept_v,
    tt,
    gs,
    loc,
    fed_v,
    p_sem,
    d_sem,
    o_sem,
    ms_sem,
    mr_sem,
    gs_sem,
    gr_sem,
    z_sem,
    k_sem,
    f_sem,
):
    R, PT, T = p_v.shape[0], p_v.shape[1], p_v.shape[2]
    D, O = d_v.shape[1], o_v.shape[1]
    S = srows.shape[1]
    CT = ccols.shape[0]
    per = R // CHUNKS
    hoff = (0, 1, G // 2)
    moff = (M - 1, 1, M // 2)
    back = (1, 0, 2)
    coff = (0, 1, G - 1, G // 2)
    B = len(hoff)
    g = lax.axis_index("group")
    m = lax.axis_index("member")
    f32, bf16 = jnp.float32, jnp.bfloat16

    o_copy = pltpu.make_async_copy(o_hbm, o_v, o_sem)
    p_copy = pltpu.make_async_copy(p_hbm, p_v, p_sem)
    p_copy.start()
    for c in range(CHUNKS):
        rows = pl.ds(c * per, per)
        pltpu.make_async_copy(d_hbm.at[rows], d_v.at[rows], d_sem.at[c]).start()
    o_copy.start()

    barrier = pltpu.get_barrier_semaphore()
    peers = [(g, lax.rem(m + d, M)) for d in moff]
    peers += [(lax.rem(g + d, G), m) for d in (1, G - 1, G // 2)]
    for peer in peers:
        pl.semaphore_signal(barrier, inc=1, device_id=peer, device_id_type=MESH)

    own = [lax.rem(g + d, G) * M + m for d in hoff]
    base = len(coff)

    sent = []
    for b in range(B):
        rel = [(hoff[b] + d) % G for d in coff]
        sent.append({s: hoff.index(r) for s, r in enumerate(rel) if r in hoff})
    relays = {1: 1, 2: 2} if G == 4 else {}
    feeds = {1: 3, 2: 0} if G == 4 else {}

    def runs(have):
        found = []
        for s in sorted(have):
            if found and sum(found[-1]) == s:
                found[-1] = (found[-1][0], found[-1][1] + 1)
            else:
                found.append((s, 1))
        return found

    def fill(b, lo, n):
        where = pl.ds(lo, n)
        return pltpu.make_async_copy(zeros.at[pl.ds(0, n)], got.at[b - 1, where], z_sem.at[b - 1, lo])

    def each_fill(act):
        for b in range(1, B):
            gap = runs(set(range(base)) - set(sent[b]))

            def some(b=b, gap=gap):
                for lo, n in gap:
                    act(fill(b, lo, n))

            if not relays:
                some()
                continue
            fed = (relays[b] + hoff[b]) % G
            other = B - b
            pl.when(jnp.logical_and(g != (relays[other] + hoff[other]) % G, g != fed))(some)

            @pl.when(g == fed)
            def _(other=other):
                act(fill(other, 0, CT))

    zeros[...] = jnp.zeros((CT, T, T), bf16)
    each_fill(lambda copy: copy.start())

    p_copy.wait()
    for f in range(R):
        parts = []
        for b in range(B):
            block = jnp.zeros((T, T), bf16)
            for q in range(PT):
                block = jnp.where(pcols[q, f] == own[b], p_v[f, q], block)
            parts.append(block)
        pm[f] = jnp.concatenate(parts, axis=1)

    for i in range(3):
        to = lax.rem(m + moff[i], M)
        for s in range(S):
            sbuf[i, s] = pm[srows[0, s, to]]

    pl.semaphore_wait(barrier, len(peers))
    m_copies = []
    for i in range(3):
        copy = pltpu.make_async_remote_copy(
            src_ref=sbuf.at[i],
            dst_ref=rbuf.at[back[i]],
            send_sem=ms_sem.at[i],
            recv_sem=mr_sem.at[back[i]],
            device_id=(g, lax.rem(m + moff[i], M)),
            device_id_type=MESH,
        )
        copy.start()
        m_copies.append(copy)

    def group_copy(b, lo, n):
        where = pl.ds(lo, n)
        return pltpu.make_async_remote_copy(
            src_ref=gs.at[b - 1, where],
            dst_ref=got.at[b - 1, where],
            send_sem=gs_sem.at[b - 1, lo],
            recv_sem=gr_sem.at[b - 1, lo],
            device_id=(lax.rem(g + hoff[b], G), m),
            device_id_type=MESH,
        )

    def feed_copy(b, lo, n):
        where = pl.ds(lo, n)
        return pltpu.make_async_remote_copy(
            src_ref=gs.at[b - 1, where],
            dst_ref=fed_v.at[where],
            send_sem=gs_sem.at[b - 1, lo],
            recv_sem=f_sem.at[lo],
            device_id=(relays[B - b], m),
            device_id_type=MESH,
        )

    cols = ((0, 1), (2,))
    spans = {
        b: [runs(s for s, b2 in sent[b].items() if b2 in part) for part in cols]
        for b in range(1, B)
    }
    half = (CT - base) // 2
    rest = [(base, half), (base + half, CT - base - half)]
    full = {b: spans[b][0] + spans[b][1] + rest for b in range(1, B)}
    alone = {b: runs(set(range(base)) - set(sent[B - b])) for b in relays}

    def each_send(b, which, act):
        def direct():
            for lo, n in which:
                act(group_copy(b, lo, n))

        if not relays:
            direct()
            return
        pl.when(jnp.logical_and(g != feeds[b], g != relays[b]))(direct)

        @pl.when(g == feeds[b])
        def _():
            for lo, n in which:
                act(feed_copy(b, lo, n))

    def start(b, which):
        each_send(b, which, lambda copy: copy.start())

    def add_and_send(b, lo, n, come):
        if come:
            feed_copy(B - b, lo, n).wait_recv()
        for s in range(lo, lo + n):
            total = None
            if s >= base:
                total = tt[spot(b, s), b * T : (b + 1) * T, :]
            elif s in sent[b]:
                total = loc[(b - 1) * T : b * T, sent[b][s] * T : (sent[b][s] + 1) * T]
            if come:
                term = fed_v[s].astype(f32)
                total = term if total is None else total + term
            gs[b - 1, s] = total.astype(bf16)
        group_copy(b, lo, n).start()

    def relay(part):
        for b in relays:

            @pl.when(g == relays[b])
            def _(b=b):
                for lo, n in rest if part == 2 else spans[B - b][part]:
                    add_and_send(b, lo, n, True)
                if part == 1:
                    for lo, n in alone[b]:
                        add_and_send(b, lo, n, False)

    def local_part(part):
        at = slice(cols[part][0] * T, (cols[part][-1] + 1) * T)
        for c in range(CHUNKS):
            if part == 0:
                rows = pl.ds(c * per, per)
                pltpu.make_async_copy(d_hbm.at[rows], d_v.at[rows], d_sem.at[c]).wait()
            for f in range(c * per, (c + 1) * per):
                left = jnp.concatenate([d_v[f, k] for k in range(D)], axis=1)
                right = jnp.concatenate([pm[dcols[k, f], :, at] for k in range(D)], axis=0)
                x[f * T : (f + 1) * T, at] = jnp.dot(
                    left, right, preferred_element_type=f32
                ).astype(bf16)
                if part == 0:
                    pmt[:, f * T : (f + 1) * T] = pm[f].T
        loc[:, at] = jnp.dot(pmt[T:, :], x[:, at], preferred_element_type=f32)

    def stage(b, part):
        for s, b2 in sent[b].items():
            if b2 in cols[part]:
                gs[b - 1, s] = loc[(b - 1) * T : b * T, b2 * T : (b2 + 1) * T].astype(bf16)

    def stage_rest(b):
        for s in range(base, CT):
            gs[b - 1, s] = tt[spot(b, s), b * T : (b + 1) * T, :].astype(bf16)

    ids = [lax.rem(m + moff[i], M) * S + s for i in range(3) for s in range(S)]
    zero = jnp.zeros((T, T), bf16)

    def remote_mid(lo, hi):
        return jnp.dot(pmt[lo:hi, :], ar[...], preferred_element_type=f32).astype(bf16)

    def remote(mid, lo, hi, arrive):
        for i in range(3):
            if arrive:
                m_copies[back[i]].wait_recv()
            res = None
            for s in range(S):
                r = i * S + s
                term = jnp.dot(
                    mid[:, r * T : (r + 1) * T], rbuf[i, s], preferred_element_type=f32
                )
                res = term if res is None else res + term
            for b2 in range(B):
                tt[i * B + b2, lo:hi] = res[:, b2 * T : (b2 + 1) * T]

    cand = [
        lax.rem(g + hoff[b2], G) * M + lax.rem(m + moff[i], M)
        for i in range(3)
        for b2 in range(B)
    ]

    def spot(b, s):
        col = ccols[s, own[b]]
        at = jnp.int32(3 * B)
        for n, c in enumerate(cand):
            at = jnp.where(col == c, n, at)
        return at

    local_part(0)
    stage(1, 0)
    start(1, spans[1][0])

    o_copy.wait()
    for f in range(R):
        for r, ident in enumerate(ids):
            block = None
            for k in range(O):
                live = jnp.logical_and(ocols[k, f] == ident, ocount[f] > k)
                term = jnp.where(live, o_v[f, k], zero)
                block = term if block is None else block + term
            ar[f * T : (f + 1) * T, r * T : (r + 1) * T] = block
    mid = remote_mid(T, B * T)
    stage(2, 0)
    start(2, spans[2][0])

    tt[3 * B] = jnp.zeros(tt.shape[1:], f32)
    remote(mid, T, B * T, True)
    stage_rest(1)
    start(1, rest)
    local_part(1)
    stage(1, 1)
    start(1, spans[1][1])
    stage_rest(2)
    start(2, rest)
    stage(2, 1)
    start(2, spans[2][1])
    relay(0)

    local = jnp.dot(pmt[:T, :], x[...], preferred_element_type=f32)
    for s in range(base):
        if s in sent[0]:
            b2 = sent[0][s]
            kept_v[s] = local[:, b2 * T : (b2 + 1) * T]
        else:
            kept_v[s] = jnp.zeros((T, T), f32)
    remote(remote_mid(0, T), 0, T, False)
    for s in range(base, CT):
        kept_v[s] = tt[spot(0, s), :T, :]
    keep = pltpu.make_async_copy(kept_v, kept, k_sem)
    keep.start()
    relay(2)
    relay(1)

    each_fill(lambda copy: copy.wait())
    keep.wait()
    for copy in m_copies:
        copy.wait_send()
    for b in range(1, B):
        each_send(b, full[b], lambda copy: copy.wait_send())
        if not relays:
            for lo, n in full[b]:
                group_copy(b, lo, n).wait_recv()
            continue
        whole = spans[B - b][0] + spans[B - b][1] + alone[b] + rest

        @pl.when(g == relays[b])
        def _(b=b, whole=whole):
            for lo, n in whole:
                group_copy(b, lo, n).wait_send()

        @pl.when(g == (relays[b] + hoff[b]) % G)
        def _(b=b, whole=whole):
            for lo, n in whole:
                group_copy(b, lo, n).wait_recv()

        @pl.when(lax.rem(g, 2) == 1)
        def _(b=b):
            for lo, n in full[b]:
                group_copy(b, lo, n).wait_recv()


def on_device(
    G,
    M,
    diag_tiles,
    diag_cols,
    offd_tiles,
    offd_cols,
    offd_count,
    p_tiles,
    p_cols,
    send_rows,
    coarse_cols,
):
    R, PT, T, _ = p_tiles.shape
    D, O = diag_tiles.shape[1], offd_tiles.shape[1]
    S = send_rows.shape[2]
    CT = coarse_cols.shape[1]
    B = 3
    bf16, f32 = jnp.bfloat16, jnp.float32
    smem = pl.BlockSpec(memory_space=pltpu.SMEM)
    hbm = pl.BlockSpec(memory_space=pl.ANY)
    kept, got = pl.pallas_call(
        functools.partial(kernel, G, M),
        out_shape=(
            jax.ShapeDtypeStruct((CT, T, T), f32),
            jax.ShapeDtypeStruct((B - 1, CT, T, T), bf16),
        ),
        in_specs=[smem] * 6 + [hbm] * 3,
        out_specs=(hbm, hbm),
        scratch_shapes=[
            pltpu.VMEM((R, PT, T, T), bf16),
            pltpu.VMEM((R, D, T, T), bf16),
            pltpu.VMEM((R, O, T, T), bf16),
            pltpu.VMEM((R, T, B * T), bf16),
            pltpu.VMEM((B * T, R * T), bf16),
            pltpu.VMEM((R * T, B * T), bf16),
            pltpu.VMEM((R * T, 3 * S * T), bf16),
            pltpu.VMEM((3, S, T, B * T), bf16),
            pltpu.VMEM((3, S, T, B * T), bf16),
            pltpu.VMEM((CT, T, T), bf16),
            pltpu.VMEM((CT, T, T), f32),
            pltpu.VMEM((3 * B + 1, B * T, T), f32),
            pltpu.VMEM((B - 1, CT, T, T), bf16),
            pltpu.VMEM(((B - 1) * T, B * T), f32),
            pltpu.VMEM((CT, T, T), bf16),
            pltpu.SemaphoreType.DMA,
            pltpu.SemaphoreType.DMA((CHUNKS,)),
            pltpu.SemaphoreType.DMA,
            pltpu.SemaphoreType.DMA((3,)),
            pltpu.SemaphoreType.DMA((3,)),
            pltpu.SemaphoreType.DMA((B - 1, CT)),
            pltpu.SemaphoreType.DMA((B - 1, CT)),
            pltpu.SemaphoreType.DMA((B - 1, CT)),
            pltpu.SemaphoreType.DMA,
            pltpu.SemaphoreType.DMA((CT,)),
        ],
        compiler_params=pltpu.CompilerParams(
            collective_id=0, has_side_effects=True, vmem_limit_bytes=63 * 1024 * 1024
        ),
    )(
        diag_cols.T,
        offd_cols.T,
        offd_count,
        p_cols.T,
        jnp.swapaxes(send_rows, 1, 2),
        coarse_cols.T,
        p_tiles,
        diag_tiles,
        offd_tiles,
    )
    return (kept + got[0].astype(f32) + got[1].astype(f32))[None]


def solution(mesh):
    return jax.shard_map(
        functools.partial(on_device, mesh.shape["group"], mesh.shape["member"]),
        mesh=mesh,
        in_specs=(
            P(("group", "member"), None, None, None),
            P(("group", "member"), None),
            P(("group", "member"), None, None, None),
            P(("group", "member"), None),
            P(("group", "member")),
            P(("group", "member"), None, None, None),
            P(("group", "member"), None),
            P(("group", "member"), None, None),
            P(),
        ),
        out_specs=P(("group", "member"), None, None, None),
        check_vma=False,
    )
```

```python
import functools

import jax
import jax.numpy as jnp
from jax import lax
from jax.experimental import pallas as pl
from jax.experimental.pallas import tpu as pltpu
from jax.sharding import PartitionSpec as P

MESH = pl.DeviceIdType.MESH
CHUNKS = 4


def kernel(
    G,
    M,
    dcols,
    ocols,
    ocount,
    pcols,
    srows,
    ccols,
    p_hbm,
    d_hbm,
    o_hbm,
    kept,
    got,
    p_v,
    d_v,
    o_v,
    pm,
    pmt,
    x,
    ar,
    sbuf,
    rbuf,
    zeros,
    kept_v,
    tt,
    gs,
    loc,
    mid,
    fed_v,
    p_sem,
    d_sem,
    o_sem,
    ms_sem,
    mr_sem,
    gs_sem,
    gr_sem,
    z_sem,
    k_sem,
    f_sem,
):
    R, PT, T = p_v.shape[0], p_v.shape[1], p_v.shape[2]
    D, O = d_v.shape[1], o_v.shape[1]
    S = srows.shape[1]
    CT = ccols.shape[0]
    per = R // CHUNKS
    hoff = (0, 1, G // 2)
    moff = (M - 1, 1, M // 2)
    back = (1, 0, 2)
    coff = (0, 1, G - 1, G // 2)
    B = len(hoff)
    g = lax.axis_index("group")
    m = lax.axis_index("member")
    f32, bf16 = jnp.float32, jnp.bfloat16

    o_copy = pltpu.make_async_copy(o_hbm, o_v, o_sem)
    p_copy = pltpu.make_async_copy(p_hbm, p_v, p_sem)
    p_copy.start()
    for c in range(CHUNKS):
        rows = pl.ds(c * per, per)
        pltpu.make_async_copy(d_hbm.at[rows], d_v.at[rows], d_sem.at[c]).start()
    o_copy.start()

    barrier = pltpu.get_barrier_semaphore()
    peers = [(g, lax.rem(m + d, M)) for d in moff]
    peers += [(lax.rem(g + d, G), m) for d in (1, G - 1, G // 2)]
    for peer in peers:
        pl.semaphore_signal(barrier, inc=1, device_id=peer, device_id_type=MESH)

    own = [lax.rem(g + d, G) * M + m for d in hoff]
    base = len(coff)

    sent = []
    for b in range(B):
        rel = [(hoff[b] + d) % G for d in coff]
        sent.append({s: hoff.index(r) for s, r in enumerate(rel) if r in hoff})
    relays = {1: 1, 2: 2} if G == 4 else {}
    feeds = {1: 3, 2: 0} if G == 4 else {}

    def runs(have):
        found = []
        for s in sorted(have):
            if found and sum(found[-1]) == s:
                found[-1] = (found[-1][0], found[-1][1] + 1)
            else:
                found.append((s, 1))
        return found

    def fill(b, lo, n):
        where = pl.ds(lo, n)
        return pltpu.make_async_copy(zeros.at[pl.ds(0, n)], got.at[b - 1, where], z_sem.at[b - 1, lo])

    def each_fill(act):
        for b in range(1, B):
            gap = runs(set(range(base)) - set(sent[b]))

            def some(b=b, gap=gap):
                for lo, n in gap:
                    act(fill(b, lo, n))

            if not relays:
                some()
                continue
            fed = (relays[b] + hoff[b]) % G
            other = B - b
            pl.when(jnp.logical_and(g != (relays[other] + hoff[other]) % G, g != fed))(some)

            @pl.when(g == fed)
            def _(other=other):
                act(fill(other, 0, CT))

    zeros[...] = jnp.zeros((CT, T, T), bf16)
    each_fill(lambda copy: copy.start())

    p_copy.wait()

    def chunks(body):
        lax.fori_loop(0, CHUNKS, lambda c, _: (body(c), 0)[1], 0)

    def chunks_behind(ahead, behind):
        ahead(0)
        lax.fori_loop(1, CHUNKS, lambda c, _: (ahead(c), behind(c - 1), 0)[2], 0)
        behind(CHUNKS - 1)

    def masked(c):
        for u in range(per):
            f = c * per + u
            parts = []
            for b in range(B):
                block = jnp.zeros((T, T), bf16)
                for q in range(PT):
                    block = jnp.where(pcols[q, f] == own[b], p_v[f, q], block)
                parts.append(block)
            pm[f] = jnp.concatenate(parts, axis=1)

    chunks(masked)

    for i in range(3):
        to = lax.rem(m + moff[i], M)
        for s in range(S):
            sbuf[i, s] = pm[srows[0, s, to]]

    pl.semaphore_wait(barrier, len(peers))
    m_copies = []
    for i in range(3):
        copy = pltpu.make_async_remote_copy(
            src_ref=sbuf.at[i],
            dst_ref=rbuf.at[back[i]],
            send_sem=ms_sem.at[i],
            recv_sem=mr_sem.at[back[i]],
            device_id=(g, lax.rem(m + moff[i], M)),
            device_id_type=MESH,
        )
        copy.start()
        m_copies.append(copy)

    def group_copy(b, lo, n):
        where = pl.ds(lo, n)
        return pltpu.make_async_remote_copy(
            src_ref=gs.at[b - 1, where],
            dst_ref=got.at[b - 1, where],
            send_sem=gs_sem.at[b - 1, lo],
            recv_sem=gr_sem.at[b - 1, lo],
            device_id=(lax.rem(g + hoff[b], G), m),
            device_id_type=MESH,
        )

    def feed_copy(b, lo, n):
        where = pl.ds(lo, n)
        return pltpu.make_async_remote_copy(
            src_ref=gs.at[b - 1, where],
            dst_ref=fed_v.at[where],
            send_sem=gs_sem.at[b - 1, lo],
            recv_sem=f_sem.at[lo],
            device_id=(relays[B - b], m),
            device_id_type=MESH,
        )

    cols = ((0, 1), (2,))
    spans = {
        b: [runs(s for s, b2 in sent[b].items() if b2 in part) for part in cols]
        for b in range(1, B)
    }
    half = (CT - base) // 2
    rest = [(base, half), (base + half, CT - base - half)]
    full = {b: spans[b][0] + spans[b][1] + rest for b in range(1, B)}
    alone = {b: runs(set(range(base)) - set(sent[B - b])) for b in relays}

    def each_send(b, which, act):
        def direct():
            for lo, n in which:
                act(group_copy(b, lo, n))

        if not relays:
            direct()
            return
        pl.when(jnp.logical_and(g != feeds[b], g != relays[b]))(direct)

        @pl.when(g == feeds[b])
        def _():
            for lo, n in which:
                act(feed_copy(b, lo, n))

    def start(b, which):
        each_send(b, which, lambda copy: copy.start())

    def add_and_send(b, lo, n, come):
        if come:
            feed_copy(B - b, lo, n).wait_recv()
        for s in range(lo, lo + n):
            total = None
            if s >= base:
                total = tt[spot(b, s), b * T : (b + 1) * T, :]
            elif s in sent[b]:
                total = loc[b * T : (b + 1) * T, sent[b][s] * T : (sent[b][s] + 1) * T]
            if come:
                term = fed_v[s].astype(f32)
                total = term if total is None else total + term
            gs[b - 1, s] = total.astype(bf16)
        group_copy(b, lo, n).start()

    def relay(part):
        for b in relays:

            @pl.when(g == relays[b])
            def _(b=b):
                for lo, n in rest if part == 2 else spans[B - b][part]:
                    add_and_send(b, lo, n, True)
                if part == 1:
                    for lo, n in alone[b]:
                        add_and_send(b, lo, n, False)

    def local_part(part):
        at = slice(cols[part][0] * T, (cols[part][-1] + 1) * T)

        def first(c):
            if part == 0:
                rows = pl.ds(c * per, per)
                pltpu.make_async_copy(d_hbm.at[rows], d_v.at[rows], d_sem.at[c]).wait()
            for u in range(per):
                f = c * per + u
                left = jnp.concatenate([d_v[f, k] for k in range(D)], axis=1)
                right = jnp.concatenate([pm[dcols[k, f], :, at] for k in range(D)], axis=0)
                x[c, u * T : (u + 1) * T, at] = jnp.dot(
                    left, right, preferred_element_type=f32
                ).astype(bf16)
                if part == 0:
                    pmt[c, :, u * T : (u + 1) * T] = pm[f].T

        def second(c):
            loc[:, at] += jnp.dot(pmt[c], x[c, :, at], preferred_element_type=f32)

        chunks_behind(first, second)

    def stage(b, part):
        for s, b2 in sent[b].items():
            if b2 in cols[part]:
                gs[b - 1, s] = loc[b * T : (b + 1) * T, b2 * T : (b2 + 1) * T].astype(bf16)

    def stage_rest(b):
        for s in range(base, CT):
            gs[b - 1, s] = tt[spot(b, s), b * T : (b + 1) * T, :].astype(bf16)

    ids = [lax.rem(m + moff[i], M) * S + s for i in range(3) for s in range(S)]
    zero = jnp.zeros((T, T), bf16)

    def spread(c):
        for u in range(per):
            f = c * per + u
            for r, ident in enumerate(ids):
                block = None
                for k in range(O):
                    live = jnp.logical_and(ocols[k, f] == ident, ocount[f] > k)
                    term = jnp.where(live, o_v[f, k], zero)
                    block = term if block is None else block + term
                ar[c, u * T : (u + 1) * T, r * T : (r + 1) * T] = block

    def gather(c):
        mid[...] += jnp.dot(pmt[c], ar[c], preferred_element_type=f32)

    def remote():
        for i in range(3):
            m_copies[back[i]].wait_recv()
            res = None
            for s in range(S):
                r = i * S + s
                term = jnp.dot(
                    mid[:, r * T : (r + 1) * T].astype(bf16),
                    rbuf[i, s],
                    preferred_element_type=f32,
                )
                res = term if res is None else res + term
            for b2 in range(B):
                tt[i * B + b2] = res[:, b2 * T : (b2 + 1) * T]

    cand = [
        lax.rem(g + hoff[b2], G) * M + lax.rem(m + moff[i], M)
        for i in range(3)
        for b2 in range(B)
    ]

    def spot(b, s):
        col = ccols[s, own[b]]
        at = jnp.int32(3 * B)
        for n, c in enumerate(cand):
            at = jnp.where(col == c, n, at)
        return at

    loc[...] = jnp.zeros(loc.shape, f32)
    mid[...] = jnp.zeros(mid.shape, f32)
    tt[3 * B] = jnp.zeros(tt.shape[1:], f32)
    local_part(0)
    stage(1, 0)
    start(1, spans[1][0])

    o_copy.wait()
    chunks_behind(spread, gather)
    stage(2, 0)
    start(2, spans[2][0])
    remote()
    stage_rest(1)
    start(1, rest)
    local_part(1)
    stage(1, 1)
    start(1, spans[1][1])
    stage_rest(2)
    start(2, rest)
    stage(2, 1)
    start(2, spans[2][1])
    relay(0)

    for s in range(base):
        if s in sent[0]:
            b2 = sent[0][s]
            kept_v[s] = loc[:T, b2 * T : (b2 + 1) * T]
        else:
            kept_v[s] = jnp.zeros((T, T), f32)
    for s in range(base, CT):
        kept_v[s] = tt[spot(0, s), :T, :]
    keep = pltpu.make_async_copy(kept_v, kept, k_sem)
    keep.start()
    relay(2)
    relay(1)

    each_fill(lambda copy: copy.wait())
    keep.wait()
    for copy in m_copies:
        copy.wait_send()
    for b in range(1, B):
        each_send(b, full[b], lambda copy: copy.wait_send())
        if not relays:
            for lo, n in full[b]:
                group_copy(b, lo, n).wait_recv()
            continue
        whole = spans[B - b][0] + spans[B - b][1] + alone[b] + rest

        @pl.when(g == relays[b])
        def _(b=b, whole=whole):
            for lo, n in whole:
                group_copy(b, lo, n).wait_send()

        @pl.when(g == (relays[b] + hoff[b]) % G)
        def _(b=b, whole=whole):
            for lo, n in whole:
                group_copy(b, lo, n).wait_recv()

        @pl.when(lax.rem(g, 2) == 1)
        def _(b=b):
            for lo, n in full[b]:
                group_copy(b, lo, n).wait_recv()


def on_device(
    G,
    M,
    diag_tiles,
    diag_cols,
    offd_tiles,
    offd_cols,
    offd_count,
    p_tiles,
    p_cols,
    send_rows,
    coarse_cols,
):
    R, PT, T, _ = p_tiles.shape
    D, O = diag_tiles.shape[1], offd_tiles.shape[1]
    S = send_rows.shape[2]
    CT = coarse_cols.shape[1]
    B = 3
    bf16, f32 = jnp.bfloat16, jnp.float32
    smem = pl.BlockSpec(memory_space=pltpu.SMEM)
    hbm = pl.BlockSpec(memory_space=pl.ANY)
    kept, got = pl.pallas_call(
        functools.partial(kernel, G, M),
        out_shape=(
            jax.ShapeDtypeStruct((CT, T, T), f32),
            jax.ShapeDtypeStruct((B - 1, CT, T, T), bf16),
        ),
        in_specs=[smem] * 6 + [hbm] * 3,
        out_specs=(hbm, hbm),
        scratch_shapes=[
            pltpu.VMEM((R, PT, T, T), bf16),
            pltpu.VMEM((R, D, T, T), bf16),
            pltpu.VMEM((R, O, T, T), bf16),
            pltpu.VMEM((R, T, B * T), bf16),
            pltpu.VMEM((CHUNKS, B * T, R // CHUNKS * T), bf16),
            pltpu.VMEM((CHUNKS, R // CHUNKS * T, B * T), bf16),
            pltpu.VMEM((CHUNKS, R // CHUNKS * T, 3 * S * T), bf16),
            pltpu.VMEM((3, S, T, B * T), bf16),
            pltpu.VMEM((3, S, T, B * T), bf16),
            pltpu.VMEM((CT, T, T), bf16),
            pltpu.VMEM((CT, T, T), f32),
            pltpu.VMEM((3 * B + 1, B * T, T), f32),
            pltpu.VMEM((B - 1, CT, T, T), bf16),
            pltpu.VMEM((B * T, B * T), f32),
            pltpu.VMEM((B * T, 3 * S * T), f32),
            pltpu.VMEM((CT, T, T), bf16),
            pltpu.SemaphoreType.DMA,
            pltpu.SemaphoreType.DMA((CHUNKS,)),
            pltpu.SemaphoreType.DMA,
            pltpu.SemaphoreType.DMA((3,)),
            pltpu.SemaphoreType.DMA((3,)),
            pltpu.SemaphoreType.DMA((B - 1, CT)),
            pltpu.SemaphoreType.DMA((B - 1, CT)),
            pltpu.SemaphoreType.DMA((B - 1, CT)),
            pltpu.SemaphoreType.DMA,
            pltpu.SemaphoreType.DMA((CT,)),
        ],
        compiler_params=pltpu.CompilerParams(
            collective_id=0, has_side_effects=True, vmem_limit_bytes=63 * 1024 * 1024
        ),
    )(
        diag_cols.T,
        offd_cols.T,
        offd_count,
        p_cols.T,
        jnp.swapaxes(send_rows, 1, 2),
        coarse_cols.T,
        p_tiles,
        diag_tiles,
        offd_tiles,
    )
    return (kept + got[0].astype(f32) + got[1].astype(f32))[None]


def solution(mesh):
    return jax.shard_map(
        functools.partial(on_device, mesh.shape["group"], mesh.shape["member"]),
        mesh=mesh,
        in_specs=(
            P(("group", "member"), None, None, None),
            P(("group", "member"), None),
            P(("group", "member"), None, None, None),
            P(("group", "member"), None),
            P(("group", "member")),
            P(("group", "member"), None, None, None),
            P(("group", "member"), None),
            P(("group", "member"), None, None),
            P(),
        ),
        out_specs=P(("group", "member"), None, None, None),
        check_vma=False,
    )
```

```python
import functools

import jax
import jax.numpy as jnp
from jax import lax
from jax.experimental import pallas as pl
from jax.experimental.pallas import tpu as pltpu
from jax.sharding import PartitionSpec as P

MESH = pl.DeviceIdType.MESH
CHUNKS = 4


def kernel(
    G,
    M,
    dcols_hbm,
    ocols_hbm,
    ocount_hbm,
    pcols_hbm,
    srows_hbm,
    ccols_hbm,
    p_hbm,
    d_hbm,
    o_hbm,
    kept,
    got,
    p_v,
    d_v,
    o_v,
    pm,
    pmt,
    x,
    ar,
    sbuf,
    rbuf,
    zeros,
    kept_v,
    tt,
    gs,
    loc,
    fed_v,
    dcols,
    ocols,
    ocount,
    pcols,
    srows,
    ccols,
    i_sem,
    p_sem,
    d_sem,
    o_sem,
    ms_sem,
    mr_sem,
    gs_sem,
    gr_sem,
    z_sem,
    k_sem,
    f_sem,
):
    R, PT, T = p_v.shape[0], p_v.shape[1], p_v.shape[2]
    D, O = d_v.shape[1], o_v.shape[1]
    S = srows.shape[1]
    CT = ccols.shape[0]
    per = R // CHUNKS
    hoff = (0, 1, G // 2)
    moff = (M - 1, 1, M // 2)
    back = (1, 0, 2)
    coff = (0, 1, G - 1, G // 2)
    B = len(hoff)
    g = lax.axis_index("group")
    m = lax.axis_index("member")
    f32, bf16 = jnp.float32, jnp.bfloat16

    ints = ((pcols_hbm, pcols), (srows_hbm, srows), (dcols_hbm, dcols))
    ints += ((ocols_hbm, ocols), (ocount_hbm, ocount), (ccols_hbm, ccols))
    i_copies = [pltpu.make_async_copy(a, b, i_sem.at[n]) for n, (a, b) in enumerate(ints)]
    for copy in i_copies:
        copy.start()
    o_copy = pltpu.make_async_copy(o_hbm, o_v, o_sem)
    p_copies = []
    for c in range(CHUNKS):
        rows = pl.ds(c * per, per)
        p_copies.append(pltpu.make_async_copy(p_hbm.at[rows], p_v.at[rows], p_sem.at[c]))
        p_copies[-1].start()
    for c in range(CHUNKS):
        rows = pl.ds(c * per, per)
        pltpu.make_async_copy(d_hbm.at[rows], d_v.at[rows], d_sem.at[c]).start()
    o_copy.start()

    barrier = pltpu.get_barrier_semaphore()
    peers = [(g, lax.rem(m + d, M)) for d in moff]
    peers += [(lax.rem(g + d, G), m) for d in (1, G - 1, G // 2)]
    for peer in peers:
        pl.semaphore_signal(barrier, inc=1, device_id=peer, device_id_type=MESH)

    own = [lax.rem(g + d, G) * M + m for d in hoff]
    base = len(coff)

    sent = []
    for b in range(B):
        rel = [(hoff[b] + d) % G for d in coff]
        sent.append({s: hoff.index(r) for s, r in enumerate(rel) if r in hoff})
    relays = {1: 1, 2: 2} if G == 4 else {}
    feeds = {1: 3, 2: 0} if G == 4 else {}

    def runs(have):
        found = []
        for s in sorted(have):
            if found and sum(found[-1]) == s:
                found[-1] = (found[-1][0], found[-1][1] + 1)
            else:
                found.append((s, 1))
        return found

    def fill(b, lo, n):
        where = pl.ds(lo, n)
        return pltpu.make_async_copy(zeros.at[pl.ds(0, n)], got.at[b - 1, where], z_sem.at[b - 1, lo])

    def each_fill(act):
        for b in range(1, B):
            gap = runs(set(range(base)) - set(sent[b]))

            def some(b=b, gap=gap):
                for lo, n in gap:
                    act(fill(b, lo, n))

            if not relays:
                some()
                continue
            fed = (relays[b] + hoff[b]) % G
            other = B - b
            pl.when(jnp.logical_and(g != (relays[other] + hoff[other]) % G, g != fed))(some)

            @pl.when(g == fed)
            def _(other=other):
                act(fill(other, 0, CT))

    zeros[...] = jnp.zeros((CT, T, T), bf16)
    each_fill(lambda copy: copy.start())

    for copy in i_copies:
        copy.wait()
    for f in range(R):
        if f % per == 0:
            p_copies[f // per].wait()
        parts = []
        for b in range(B):
            block = jnp.zeros((T, T), bf16)
            for q in range(PT):
                block = jnp.where(pcols[q, f] == own[b], p_v[f, q], block)
            parts.append(block)
        pm[f] = jnp.concatenate(parts, axis=1)

    for i in range(3):
        to = lax.rem(m + moff[i], M)
        for s in range(S):
            sbuf[i, s] = pm[srows[0, s, to]]

    m_copies = [
        pltpu.make_async_remote_copy(
            src_ref=sbuf.at[i],
            dst_ref=rbuf.at[back[i]],
            send_sem=ms_sem.at[i],
            recv_sem=mr_sem.at[back[i]],
            device_id=(g, lax.rem(m + moff[i], M)),
            device_id_type=MESH,
        )
        for i in range(3)
    ]

    def enter():
        pl.semaphore_wait(barrier, len(peers))
        for copy in m_copies:
            copy.start()

    def group_copy(b, lo, n):
        where = pl.ds(lo, n)
        return pltpu.make_async_remote_copy(
            src_ref=gs.at[b - 1, where],
            dst_ref=got.at[b - 1, where],
            send_sem=gs_sem.at[b - 1, lo],
            recv_sem=gr_sem.at[b - 1, lo],
            device_id=(lax.rem(g + hoff[b], G), m),
            device_id_type=MESH,
        )

    def feed_copy(b, lo, n):
        where = pl.ds(lo, n)
        return pltpu.make_async_remote_copy(
            src_ref=gs.at[b - 1, where],
            dst_ref=fed_v.at[where],
            send_sem=gs_sem.at[b - 1, lo],
            recv_sem=f_sem.at[lo],
            device_id=(relays[B - b], m),
            device_id_type=MESH,
        )

    cols = ((0, 1), (2,))
    spans = {
        b: [runs(s for s, b2 in sent[b].items() if b2 in part) for part in cols]
        for b in range(1, B)
    }
    half = (CT - base) // 2
    rest = [(base, half), (base + half, CT - base - half)]
    full = {b: spans[b][0] + spans[b][1] + rest for b in range(1, B)}
    alone = {b: runs(set(range(base)) - set(sent[B - b])) for b in relays}

    def each_send(b, which, act):
        def direct():
            for lo, n in which:
                act(group_copy(b, lo, n))

        if not relays:
            direct()
            return
        pl.when(jnp.logical_and(g != feeds[b], g != relays[b]))(direct)

        @pl.when(g == feeds[b])
        def _():
            for lo, n in which:
                act(feed_copy(b, lo, n))

    def start(b, which):
        each_send(b, which, lambda copy: copy.start())

    def add_and_send(b, lo, n, come):
        if come:
            feed_copy(B - b, lo, n).wait_recv()
        for s in range(lo, lo + n):
            total = None
            if s >= base:
                total = tt[spot(b, s), b * T : (b + 1) * T, :]
            elif s in sent[b]:
                total = loc[(b - 1) * T : b * T, sent[b][s] * T : (sent[b][s] + 1) * T]
            if come:
                term = fed_v[s].astype(f32)
                total = term if total is None else total + term
            gs[b - 1, s] = total.astype(bf16)
        group_copy(b, lo, n).start()

    def relay(part):
        for b in relays:

            @pl.when(g == relays[b])
            def _(b=b):
                for lo, n in rest if part == 2 else spans[B - b][part]:
                    add_and_send(b, lo, n, True)
                if part == 1:
                    for lo, n in alone[b]:
                        add_and_send(b, lo, n, False)

    def local_part(part):
        at = slice(cols[part][0] * T, (cols[part][-1] + 1) * T)
        for c in range(CHUNKS):
            if part == 0:
                rows = pl.ds(c * per, per)
                pltpu.make_async_copy(d_hbm.at[rows], d_v.at[rows], d_sem.at[c]).wait()
            for f in range(c * per, (c + 1) * per):
                left = jnp.concatenate([d_v[f, k] for k in range(D)], axis=1)
                right = jnp.concatenate([pm[dcols[k, f], :, at] for k in range(D)], axis=0)
                x[f * T : (f + 1) * T, at] = jnp.dot(
                    left, right, preferred_element_type=f32
                ).astype(bf16)
                if part == 0:
                    pmt[:, f * T : (f + 1) * T] = pm[f].T
            if part == 0 and c == CHUNKS - 2:
                enter()
        loc[:, at] = jnp.dot(pmt[T:, :], x[:, at], preferred_element_type=f32)

    def stage(b, part):
        for s, b2 in sent[b].items():
            if b2 in cols[part]:
                gs[b - 1, s] = loc[(b - 1) * T : b * T, b2 * T : (b2 + 1) * T].astype(bf16)

    def stage_rest(b):
        for s in range(base, CT):
            gs[b - 1, s] = tt[spot(b, s), b * T : (b + 1) * T, :].astype(bf16)

    ids = [lax.rem(m + moff[i], M) * S + s for i in range(3) for s in range(S)]
    zero = jnp.zeros((T, T), bf16)

    def remote_mid(lo, hi):
        return jnp.dot(pmt[lo:hi, :], ar[...], preferred_element_type=f32).astype(bf16)

    def remote(mid, lo, hi, arrive):
        for i in range(3):
            if arrive:
                m_copies[back[i]].wait_recv()
            res = None
            for s in range(S):
                r = i * S + s
                term = jnp.dot(
                    mid[:, r * T : (r + 1) * T], rbuf[i, s], preferred_element_type=f32
                )
                res = term if res is None else res + term
            for b2 in range(B):
                tt[i * B + b2, lo:hi] = res[:, b2 * T : (b2 + 1) * T]

    cand = [
        lax.rem(g + hoff[b2], G) * M + lax.rem(m + moff[i], M)
        for i in range(3)
        for b2 in range(B)
    ]

    def spot(b, s):
        col = ccols[s, own[b]]
        at = jnp.int32(3 * B)
        for n, c in enumerate(cand):
            at = jnp.where(col == c, n, at)
        return at

    local_part(0)
    stage(1, 0)
    start(1, spans[1][0])

    o_copy.wait()
    for f in range(R):
        for r, ident in enumerate(ids):
            block = None
            for k in range(O):
                live = jnp.logical_and(ocols[k, f] == ident, ocount[f] > k)
                term = jnp.where(live, o_v[f, k], zero)
                block = term if block is None else block + term
            ar[f * T : (f + 1) * T, r * T : (r + 1) * T] = block
    mid = remote_mid(T, B * T)
    stage(2, 0)
    start(2, spans[2][0])

    tt[3 * B] = jnp.zeros(tt.shape[1:], f32)
    remote(mid, T, B * T, True)
    stage_rest(1)
    start(1, rest)
    local_part(1)
    stage(1, 1)
    start(1, spans[1][1])
    stage_rest(2)
    start(2, rest)
    stage(2, 1)
    start(2, spans[2][1])
    relay(0)

    local = jnp.dot(pmt[:T, :], x[...], preferred_element_type=f32)
    for s in range(base):
        if s in sent[0]:
            b2 = sent[0][s]
            kept_v[s] = local[:, b2 * T : (b2 + 1) * T]
        else:
            kept_v[s] = jnp.zeros((T, T), f32)
    relay(2)
    relay(1)
    remote(remote_mid(0, T), 0, T, False)
    for s in range(base, CT):
        kept_v[s] = tt[spot(0, s), :T, :]
    keep = pltpu.make_async_copy(kept_v, kept, k_sem)
    keep.start()

    each_fill(lambda copy: copy.wait())
    keep.wait()
    for copy in m_copies:
        copy.wait_send()
    for b in range(1, B):
        each_send(b, full[b], lambda copy: copy.wait_send())
        if not relays:
            for lo, n in full[b]:
                group_copy(b, lo, n).wait_recv()
            continue
        whole = spans[B - b][0] + spans[B - b][1] + alone[b] + rest

        @pl.when(g == relays[b])
        def _(b=b, whole=whole):
            for lo, n in whole:
                group_copy(b, lo, n).wait_send()

        @pl.when(g == (relays[b] + hoff[b]) % G)
        def _(b=b, whole=whole):
            for lo, n in whole:
                group_copy(b, lo, n).wait_recv()

        @pl.when(lax.rem(g, 2) == 1)
        def _(b=b):
            for lo, n in full[b]:
                group_copy(b, lo, n).wait_recv()


def on_device(
    G,
    M,
    diag_tiles,
    diag_cols,
    offd_tiles,
    offd_cols,
    offd_count,
    p_tiles,
    p_cols,
    send_rows,
    coarse_cols,
):
    R, PT, T, _ = p_tiles.shape
    D, O = diag_tiles.shape[1], offd_tiles.shape[1]
    S = send_rows.shape[2]
    CT = coarse_cols.shape[1]
    B = 3
    bf16, f32 = jnp.bfloat16, jnp.float32
    i32 = jnp.int32
    hbm = pl.BlockSpec(memory_space=pl.ANY)
    kept, got = pl.pallas_call(
        functools.partial(kernel, G, M),
        out_shape=(
            jax.ShapeDtypeStruct((CT, T, T), f32),
            jax.ShapeDtypeStruct((B - 1, CT, T, T), bf16),
        ),
        in_specs=[hbm] * 9,
        out_specs=(hbm, hbm),
        scratch_shapes=[
            pltpu.VMEM((R, PT, T, T), bf16),
            pltpu.VMEM((R, D, T, T), bf16),
            pltpu.VMEM((R, O, T, T), bf16),
            pltpu.VMEM((R, T, B * T), bf16),
            pltpu.VMEM((B * T, R * T), bf16),
            pltpu.VMEM((R * T, B * T), bf16),
            pltpu.VMEM((R * T, 3 * S * T), bf16),
            pltpu.VMEM((3, S, T, B * T), bf16),
            pltpu.VMEM((3, S, T, B * T), bf16),
            pltpu.VMEM((CT, T, T), bf16),
            pltpu.VMEM((CT, T, T), f32),
            pltpu.VMEM((3 * B + 1, B * T, T), f32),
            pltpu.VMEM((B - 1, CT, T, T), bf16),
            pltpu.VMEM(((B - 1) * T, B * T), f32),
            pltpu.VMEM((CT, T, T), bf16),
            pltpu.SMEM((D, R), i32),
            pltpu.SMEM((O, R), i32),
            pltpu.SMEM((R,), i32),
            pltpu.SMEM((PT, R), i32),
            pltpu.SMEM((1, S, send_rows.shape[1]), i32),
            pltpu.SMEM((CT, coarse_cols.shape[0]), i32),
            pltpu.SemaphoreType.DMA((6,)),
            pltpu.SemaphoreType.DMA((CHUNKS,)),
            pltpu.SemaphoreType.DMA((CHUNKS,)),
            pltpu.SemaphoreType.DMA,
            pltpu.SemaphoreType.DMA((3,)),
            pltpu.SemaphoreType.DMA((3,)),
            pltpu.SemaphoreType.DMA((B - 1, CT)),
            pltpu.SemaphoreType.DMA((B - 1, CT)),
            pltpu.SemaphoreType.DMA((B - 1, CT)),
            pltpu.SemaphoreType.DMA,
            pltpu.SemaphoreType.DMA((CT,)),
        ],
        compiler_params=pltpu.CompilerParams(
            collective_id=0, has_side_effects=True, vmem_limit_bytes=63 * 1024 * 1024
        ),
    )(
        diag_cols.T,
        offd_cols.T,
        offd_count,
        p_cols.T,
        jnp.swapaxes(send_rows, 1, 2),
        coarse_cols.T,
        p_tiles,
        diag_tiles,
        offd_tiles,
    )
    return (kept + got[0].astype(f32) + got[1].astype(f32))[None]


def solution(mesh):
    return jax.shard_map(
        functools.partial(on_device, mesh.shape["group"], mesh.shape["member"]),
        mesh=mesh,
        in_specs=(
            P(("group", "member"), None, None, None),
            P(("group", "member"), None),
            P(("group", "member"), None, None, None),
            P(("group", "member"), None),
            P(("group", "member")),
            P(("group", "member"), None, None, None),
            P(("group", "member"), None),
            P(("group", "member"), None, None),
            P(),
        ),
        out_specs=P(("group", "member"), None, None, None),
        check_vma=False,
    )
```

```python
import functools

import jax
import jax.numpy as jnp
from jax import lax
from jax.experimental import pallas as pl
from jax.experimental.pallas import tpu as pltpu
from jax.sharding import PartitionSpec as P

MESH = pl.DeviceIdType.MESH
CHUNKS = 4


def kernel(
    G,
    M,
    dcols_hbm,
    ocols_hbm,
    ocount_hbm,
    pcols_hbm,
    srows_hbm,
    ccols_hbm,
    p_hbm,
    d_hbm,
    o_hbm,
    kept,
    got,
    p_v,
    d_v,
    o_v,
    pm,
    pmt,
    x,
    ar,
    sbuf,
    rbuf,
    zeros,
    kept_v,
    tt,
    gs,
    loc,
    fed_v,
    dcols,
    ocols,
    ocount,
    pcols,
    srows,
    ccols,
    i_sem,
    p_sem,
    d_sem,
    o_sem,
    ms_sem,
    mr_sem,
    gs_sem,
    gr_sem,
    z_sem,
    k_sem,
    f_sem,
):
    R, PT, T = p_v.shape[0], p_v.shape[1], p_v.shape[2]
    D, O = d_v.shape[1], o_v.shape[1]
    S = srows.shape[1]
    CT = ccols.shape[0]
    per = R // CHUNKS
    hoff = (0, 1, G // 2)
    moff = (M - 1, 1, M // 2)
    back = (1, 0, 2)
    coff = (0, 1, G - 1, G // 2)
    B = len(hoff)
    g = lax.axis_index("group")
    m = lax.axis_index("member")
    f32, bf16 = jnp.float32, jnp.bfloat16

    ints = ((pcols_hbm, pcols), (srows_hbm, srows), (dcols_hbm, dcols))
    ints += ((ocols_hbm, ocols), (ocount_hbm, ocount), (ccols_hbm, ccols))
    i_copies = [pltpu.make_async_copy(a, b, i_sem.at[n]) for n, (a, b) in enumerate(ints)]
    for copy in i_copies:
        copy.start()
    o_copy = pltpu.make_async_copy(o_hbm, o_v, o_sem)
    p_copies = []
    for c in range(CHUNKS):
        rows = pl.ds(c * per, per)
        p_copies.append(pltpu.make_async_copy(p_hbm.at[rows], p_v.at[rows], p_sem.at[c]))
        p_copies[-1].start()
    for c in range(CHUNKS):
        rows = pl.ds(c * per, per)
        pltpu.make_async_copy(d_hbm.at[rows], d_v.at[rows], d_sem.at[c]).start()
    o_copy.start()

    barrier = pltpu.get_barrier_semaphore()
    peers = [(g, lax.rem(m + d, M)) for d in moff]
    peers += [(lax.rem(g + d, G), m) for d in (1, G - 1, G // 2)]
    for peer in peers:
        pl.semaphore_signal(barrier, inc=1, device_id=peer, device_id_type=MESH)

    own = [lax.rem(g + d, G) * M + m for d in hoff]
    base = len(coff)

    sent = []
    for b in range(B):
        rel = [(hoff[b] + d) % G for d in coff]
        sent.append({s: hoff.index(r) for s, r in enumerate(rel) if r in hoff})
    relays = {1: 1, 2: 2} if G == 4 else {}
    feeds = {1: 3, 2: 0} if G == 4 else {}

    def runs(have):
        found = []
        for s in sorted(have):
            if found and sum(found[-1]) == s:
                found[-1] = (found[-1][0], found[-1][1] + 1)
            else:
                found.append((s, 1))
        return found

    def fill(b, lo, n):
        where = pl.ds(lo, n)
        return pltpu.make_async_copy(zeros.at[pl.ds(0, n)], got.at[b - 1, where], z_sem.at[b - 1, lo])

    def each_fill(act):
        for b in range(1, B):
            gap = runs(set(range(base)) - set(sent[b]))

            def some(b=b, gap=gap):
                for lo, n in gap:
                    act(fill(b, lo, n))

            some()
            if not relays:
                continue
            other = B - b

            @pl.when(g == (relays[b] + hoff[b]) % G)
            def _(other=other):
                act(fill(other, base, CT - base))

    zeros[...] = jnp.zeros((CT, T, T), bf16)
    each_fill(lambda copy: copy.start())

    for copy in i_copies:
        copy.wait()
    for f in range(R):
        if f % per == 0:
            p_copies[f // per].wait()
        parts = []
        for b in range(B):
            block = jnp.zeros((T, T), bf16)
            for q in range(PT):
                block = jnp.where(pcols[q, f] == own[b], p_v[f, q], block)
            parts.append(block)
        pm[f] = jnp.concatenate(parts, axis=1)

    for i in range(3):
        to = lax.rem(m + moff[i], M)
        for s in range(S):
            sbuf[i, s] = pm[srows[0, s, to]]

    m_copies = [
        pltpu.make_async_remote_copy(
            src_ref=sbuf.at[i],
            dst_ref=rbuf.at[back[i]],
            send_sem=ms_sem.at[i],
            recv_sem=mr_sem.at[back[i]],
            device_id=(g, lax.rem(m + moff[i], M)),
            device_id_type=MESH,
        )
        for i in range(3)
    ]

    def enter():
        pl.semaphore_wait(barrier, len(peers))
        for copy in m_copies:
            copy.start()

    def group_copy(b, lo, n):
        where = pl.ds(lo, n)
        return pltpu.make_async_remote_copy(
            src_ref=gs.at[b - 1, where],
            dst_ref=got.at[b - 1, where],
            send_sem=gs_sem.at[b - 1, lo],
            recv_sem=gr_sem.at[b - 1, lo],
            device_id=(lax.rem(g + hoff[b], G), m),
            device_id_type=MESH,
        )

    def feed_copy(b, lo, n):
        where = pl.ds(lo, n)
        return pltpu.make_async_remote_copy(
            src_ref=gs.at[b - 1, where],
            dst_ref=fed_v.at[where],
            send_sem=gs_sem.at[b - 1, lo],
            recv_sem=f_sem.at[lo],
            device_id=(relays[B - b], m),
            device_id_type=MESH,
        )

    cols = ((0, 1), (2,))
    spans = {
        b: [runs(s for s, b2 in sent[b].items() if b2 in part) for part in cols]
        for b in range(1, B)
    }
    half = (CT - base) // 2
    rest = [(base, half), (base + half, CT - base - half)]
    def each_send(b, which, act):
        def direct():
            for lo, n in which:
                act(group_copy(b, lo, n))

        if not relays or which is not rest:
            direct()
            return
        pl.when(jnp.logical_and(g != feeds[b], g != relays[b]))(direct)

        @pl.when(g == feeds[b])
        def _():
            for lo, n in which:
                act(feed_copy(b, lo, n))

    def start(b, which):
        each_send(b, which, lambda copy: copy.start())

    def add_and_send(b, lo, n):
        feed_copy(B - b, lo, n).wait_recv()
        for s in range(lo, lo + n):
            total = tt[spot(b, s), b * T : (b + 1) * T, :] + fed_v[s].astype(f32)
            gs[b - 1, s] = total.astype(bf16)
        group_copy(b, lo, n).start()

    def relay():
        for b in relays:

            @pl.when(g == relays[b])
            def _(b=b):
                for lo, n in rest:
                    add_and_send(b, lo, n)

    def local_part(part):
        at = slice(cols[part][0] * T, (cols[part][-1] + 1) * T)
        for c in range(CHUNKS):
            if part == 0:
                rows = pl.ds(c * per, per)
                pltpu.make_async_copy(d_hbm.at[rows], d_v.at[rows], d_sem.at[c]).wait()
            for f in range(c * per, (c + 1) * per):
                left = jnp.concatenate([d_v[f, k] for k in range(D)], axis=1)
                right = jnp.concatenate([pm[dcols[k, f], :, at] for k in range(D)], axis=0)
                x[f * T : (f + 1) * T, at] = jnp.dot(
                    left, right, preferred_element_type=f32
                ).astype(bf16)
                if part == 0:
                    pmt[:, f * T : (f + 1) * T] = pm[f].T
            if part == 0 and c == CHUNKS - 2:
                enter()
        loc[:, at] = jnp.dot(pmt[T:, :], x[:, at], preferred_element_type=f32)

    def stage(b, part):
        for s, b2 in sent[b].items():
            if b2 in cols[part]:
                gs[b - 1, s] = loc[(b - 1) * T : b * T, b2 * T : (b2 + 1) * T].astype(bf16)

    def stage_rest(b):
        for s in range(base, CT):
            gs[b - 1, s] = tt[spot(b, s), b * T : (b + 1) * T, :].astype(bf16)

    ids = [lax.rem(m + moff[i], M) * S + s for i in range(3) for s in range(S)]
    zero = jnp.zeros((T, T), bf16)

    def remote_mid(lo, hi):
        return jnp.dot(pmt[lo:hi, :], ar[...], preferred_element_type=f32).astype(bf16)

    def remote(mid, lo, hi, arrive):
        for i in range(3):
            if arrive:
                m_copies[back[i]].wait_recv()
            res = None
            for s in range(S):
                r = i * S + s
                term = jnp.dot(
                    mid[:, r * T : (r + 1) * T], rbuf[i, s], preferred_element_type=f32
                )
                res = term if res is None else res + term
            for b2 in range(B):
                tt[i * B + b2, lo:hi] = res[:, b2 * T : (b2 + 1) * T]

    cand = [
        lax.rem(g + hoff[b2], G) * M + lax.rem(m + moff[i], M)
        for i in range(3)
        for b2 in range(B)
    ]

    def spot(b, s):
        col = ccols[s, own[b]]
        at = jnp.int32(3 * B)
        for n, c in enumerate(cand):
            at = jnp.where(col == c, n, at)
        return at

    local_part(0)
    for b in (1, 2):
        stage(b, 0)
        start(b, spans[b][0])

    o_copy.wait()
    for f in range(R):
        for r, ident in enumerate(ids):
            block = None
            for k in range(O):
                live = jnp.logical_and(ocols[k, f] == ident, ocount[f] > k)
                term = jnp.where(live, o_v[f, k], zero)
                block = term if block is None else block + term
            ar[f * T : (f + 1) * T, r * T : (r + 1) * T] = block
    mid = remote_mid(T, B * T)

    tt[3 * B] = jnp.zeros(tt.shape[1:], f32)
    remote(mid, T, B * T, True)
    stage_rest(1)
    start(1, rest)
    local_part(1)
    stage(1, 1)
    start(1, spans[1][1])
    stage_rest(2)
    start(2, rest)
    stage(2, 1)
    start(2, spans[2][1])

    local = jnp.dot(pmt[:T, :], x[...], preferred_element_type=f32)
    for s in range(base):
        if s in sent[0]:
            b2 = sent[0][s]
            kept_v[s] = local[:, b2 * T : (b2 + 1) * T]
        else:
            kept_v[s] = jnp.zeros((T, T), f32)
    relay()
    remote(remote_mid(0, T), 0, T, False)
    for s in range(base, CT):
        kept_v[s] = tt[spot(0, s), :T, :]
    keep = pltpu.make_async_copy(kept_v, kept, k_sem)
    keep.start()

    each_fill(lambda copy: copy.wait())
    keep.wait()
    for copy in m_copies:
        copy.wait_send()
    for b in range(1, B):
        for which in spans[b] + [rest]:
            each_send(b, which, lambda copy: copy.wait_send())
        for lo, n in spans[b][0] + spans[b][1]:
            group_copy(b, lo, n).wait_recv()

        def last(b=b):
            for lo, n in rest:
                group_copy(b, lo, n).wait_recv()

        if not relays:
            last()
            continue

        @pl.when(g == relays[b])
        def _(b=b):
            for lo, n in rest:
                group_copy(b, lo, n).wait_send()

        to = (relays[b] + hoff[b]) % G
        pl.when(jnp.logical_or(g == to, lax.rem(g, 2) == 1))(last)


def on_device(
    G,
    M,
    diag_tiles,
    diag_cols,
    offd_tiles,
    offd_cols,
    offd_count,
    p_tiles,
    p_cols,
    send_rows,
    coarse_cols,
):
    R, PT, T, _ = p_tiles.shape
    D, O = diag_tiles.shape[1], offd_tiles.shape[1]
    S = send_rows.shape[2]
    CT = coarse_cols.shape[1]
    B = 3
    bf16, f32 = jnp.bfloat16, jnp.float32
    i32 = jnp.int32
    hbm = pl.BlockSpec(memory_space=pl.ANY)
    kept, got = pl.pallas_call(
        functools.partial(kernel, G, M),
        out_shape=(
            jax.ShapeDtypeStruct((CT, T, T), f32),
            jax.ShapeDtypeStruct((B - 1, CT, T, T), bf16),
        ),
        in_specs=[hbm] * 9,
        out_specs=(hbm, hbm),
        scratch_shapes=[
            pltpu.VMEM((R, PT, T, T), bf16),
            pltpu.VMEM((R, D, T, T), bf16),
            pltpu.VMEM((R, O, T, T), bf16),
            pltpu.VMEM((R, T, B * T), bf16),
            pltpu.VMEM((B * T, R * T), bf16),
            pltpu.VMEM((R * T, B * T), bf16),
            pltpu.VMEM((R * T, 3 * S * T), bf16),
            pltpu.VMEM((3, S, T, B * T), bf16),
            pltpu.VMEM((3, S, T, B * T), bf16),
            pltpu.VMEM((CT, T, T), bf16),
            pltpu.VMEM((CT, T, T), f32),
            pltpu.VMEM((3 * B + 1, B * T, T), f32),
            pltpu.VMEM((B - 1, CT, T, T), bf16),
            pltpu.VMEM(((B - 1) * T, B * T), f32),
            pltpu.VMEM((CT, T, T), bf16),
            pltpu.SMEM((D, R), i32),
            pltpu.SMEM((O, R), i32),
            pltpu.SMEM((R,), i32),
            pltpu.SMEM((PT, R), i32),
            pltpu.SMEM((1, S, send_rows.shape[1]), i32),
            pltpu.SMEM((CT, coarse_cols.shape[0]), i32),
            pltpu.SemaphoreType.DMA((6,)),
            pltpu.SemaphoreType.DMA((CHUNKS,)),
            pltpu.SemaphoreType.DMA((CHUNKS,)),
            pltpu.SemaphoreType.DMA,
            pltpu.SemaphoreType.DMA((3,)),
            pltpu.SemaphoreType.DMA((3,)),
            pltpu.SemaphoreType.DMA((B - 1, CT)),
            pltpu.SemaphoreType.DMA((B - 1, CT)),
            pltpu.SemaphoreType.DMA((B - 1, CT)),
            pltpu.SemaphoreType.DMA,
            pltpu.SemaphoreType.DMA((CT,)),
        ],
        compiler_params=pltpu.CompilerParams(
            collective_id=0, has_side_effects=True, vmem_limit_bytes=63 * 1024 * 1024
        ),
    )(
        diag_cols.T,
        offd_cols.T,
        offd_count,
        p_cols.T,
        jnp.swapaxes(send_rows, 1, 2),
        coarse_cols.T,
        p_tiles,
        diag_tiles,
        offd_tiles,
    )
    return (kept + got[0].astype(f32) + got[1].astype(f32))[None]


def solution(mesh):
    return jax.shard_map(
        functools.partial(on_device, mesh.shape["group"], mesh.shape["member"]),
        mesh=mesh,
        in_specs=(
            P(("group", "member"), None, None, None),
            P(("group", "member"), None),
            P(("group", "member"), None, None, None),
            P(("group", "member"), None),
            P(("group", "member")),
            P(("group", "member"), None, None, None),
            P(("group", "member"), None),
            P(("group", "member"), None, None),
            P(),
        ),
        out_specs=P(("group", "member"), None, None, None),
        check_vma=False,
    )
```

```python
import functools

import jax
import jax.numpy as jnp
from jax import lax
from jax.experimental import pallas as pl
from jax.experimental.pallas import tpu as pltpu
from jax.sharding import PartitionSpec as P

MESH = pl.DeviceIdType.MESH
CHUNKS = 4


def kernel(
    G,
    M,
    dcols_hbm,
    ocols_hbm,
    ocount_hbm,
    pcols_hbm,
    srows_hbm,
    ccols_hbm,
    p_hbm,
    d_hbm,
    o_hbm,
    kept,
    got,
    p_v,
    d_v,
    o_v,
    pm,
    pmt,
    x,
    ar,
    sbuf,
    rbuf,
    zeros,
    kept_v,
    tt,
    gs,
    loc,
    fed_v,
    dcols,
    ocols,
    ocount,
    pcols,
    srows,
    ccols,
    i_sem,
    p_sem,
    d_sem,
    o_sem,
    ms_sem,
    mr_sem,
    gs_sem,
    gr_sem,
    z_sem,
    k_sem,
    f_sem,
):
    R, PT, T = p_v.shape[0], p_v.shape[1], p_v.shape[2]
    D, O = d_v.shape[1], o_v.shape[1]
    S = srows.shape[1]
    CT = ccols.shape[0]
    per = R // CHUNKS
    hoff = (0, 1, G // 2)
    moff = (M - 1, 1, M // 2)
    back = (1, 0, 2)
    coff = (0, 1, G - 1, G // 2)
    B = len(hoff)
    g = lax.axis_index("group")
    m = lax.axis_index("member")
    f32, bf16 = jnp.float32, jnp.bfloat16

    ints = ((pcols_hbm, pcols), (srows_hbm, srows), (dcols_hbm, dcols))
    ints += ((ocols_hbm, ocols), (ocount_hbm, ocount), (ccols_hbm, ccols))
    i_copies = [pltpu.make_async_copy(a, b, i_sem.at[n]) for n, (a, b) in enumerate(ints)]
    for copy in i_copies:
        copy.start()
    o_copy = pltpu.make_async_copy(o_hbm, o_v, o_sem)
    p_copies = []
    for c in range(CHUNKS):
        rows = pl.ds(c * per, per)
        p_copies.append(pltpu.make_async_copy(p_hbm.at[rows], p_v.at[rows], p_sem.at[c]))
        p_copies[-1].start()
    for c in range(CHUNKS):
        rows = pl.ds(c * per, per)
        pltpu.make_async_copy(d_hbm.at[rows], d_v.at[rows], d_sem.at[c]).start()
    o_copy.start()

    barrier = pltpu.get_barrier_semaphore()
    peers = [(g, lax.rem(m + d, M)) for d in moff]
    peers += [(lax.rem(g + d, G), m) for d in (1, G - 1, G // 2)]
    for peer in peers:
        pl.semaphore_signal(barrier, inc=1, device_id=peer, device_id_type=MESH)

    own = [lax.rem(g + d, G) * M + m for d in hoff]
    base = len(coff)

    sent = []
    for b in range(B):
        rel = [(hoff[b] + d) % G for d in coff]
        sent.append({s: hoff.index(r) for s, r in enumerate(rel) if r in hoff})
    relays = {1: 1, 2: 2} if G == 4 else {}
    feeds = {1: 3, 2: 0} if G == 4 else {}

    def runs(have):
        found = []
        for s in sorted(have):
            if found and sum(found[-1]) == s:
                found[-1] = (found[-1][0], found[-1][1] + 1)
            else:
                found.append((s, 1))
        return found

    def fill(b, lo, n):
        where = pl.ds(lo, n)
        return pltpu.make_async_copy(zeros.at[pl.ds(0, n)], got.at[b - 1, where], z_sem.at[b - 1, lo])

    def each_fill(act):
        for b in range(1, B):
            gap = runs(set(range(base)) - set(sent[b]))

            def some(b=b, gap=gap):
                for lo, n in gap:
                    act(fill(b, lo, n))

            some()
            if not relays:
                continue
            other = B - b

            @pl.when(g == (relays[b] + hoff[b]) % G)
            def _(other=other):
                act(fill(other, base, CT - base))

    zeros[...] = jnp.zeros((CT, T, T), bf16)
    each_fill(lambda copy: copy.start())

    for copy in i_copies:
        copy.wait()
    for f in range(R):
        if f % per == 0:
            p_copies[f // per].wait()
        parts = []
        for b in range(B):
            block = jnp.zeros((T, T), bf16)
            for q in range(PT):
                block = jnp.where(pcols[q, f] == own[b], p_v[f, q], block)
            parts.append(block)
        pm[f] = jnp.concatenate(parts, axis=1)

    for i in range(3):
        to = lax.rem(m + moff[i], M)
        for s in range(S):
            sbuf[i, s] = pm[srows[0, s, to]]

    m_copies = [
        pltpu.make_async_remote_copy(
            src_ref=sbuf.at[i],
            dst_ref=rbuf.at[back[i]],
            send_sem=ms_sem.at[i],
            recv_sem=mr_sem.at[back[i]],
            device_id=(g, lax.rem(m + moff[i], M)),
            device_id_type=MESH,
        )
        for i in range(3)
    ]

    def enter():
        pl.semaphore_wait(barrier, len(peers))
        for copy in m_copies:
            copy.start()

    def group_copy(b, lo, n):
        where = pl.ds(lo, n)
        return pltpu.make_async_remote_copy(
            src_ref=gs.at[b - 1, where],
            dst_ref=got.at[b - 1, where],
            send_sem=gs_sem.at[b - 1, lo],
            recv_sem=gr_sem.at[b - 1, lo],
            device_id=(lax.rem(g + hoff[b], G), m),
            device_id_type=MESH,
        )

    def feed_copy(b, lo, n):
        where = pl.ds(lo, n)
        return pltpu.make_async_remote_copy(
            src_ref=gs.at[b - 1, where],
            dst_ref=fed_v.at[where],
            send_sem=gs_sem.at[b - 1, lo],
            recv_sem=f_sem.at[lo],
            device_id=(relays[B - b], m),
            device_id_type=MESH,
        )

    cols = ((0, 1), (2,))
    spans = {
        b: [runs(s for s, b2 in sent[b].items() if b2 in part) for part in cols]
        for b in range(1, B)
    }
    rest = [(s, 1) for s in range(base, CT)]

    def each_send(b, which, act):
        def direct():
            for lo, n in which:
                act(group_copy(b, lo, n))

        if not relays or which is not rest:
            direct()
            return
        pl.when(jnp.logical_and(g != feeds[b], g != relays[b]))(direct)

        @pl.when(g == feeds[b])
        def _():
            for lo, n in which:
                act(feed_copy(b, lo, n))

    def start(b, which):
        each_send(b, which, lambda copy: copy.start())

    def start_feeds():
        for b in relays:

            @pl.when(g == feeds[b])
            def _(b=b):
                for lo, n in rest:
                    feed_copy(b, lo, n).start()

    def start_rest(b):
        def direct():
            for lo, n in rest:
                group_copy(b, lo, n).start()

        if relays:
            pl.when(jnp.logical_and(g != feeds[b], g != relays[b]))(direct)
        else:
            direct()

    def add_and_send(b, lo, n):
        feed_copy(B - b, lo, n).wait_recv()
        for s in range(lo, lo + n):
            total = tt[spot(b, s), b * T : (b + 1) * T, :] + fed_v[s].astype(f32)
            gs[b - 1, s] = total.astype(bf16)
        group_copy(b, lo, n).start()

    def relay():
        for b in relays:

            @pl.when(g == relays[b])
            def _(b=b):
                for lo, n in rest:
                    add_and_send(b, lo, n)

    def local_part(part):
        at = slice(cols[part][0] * T, (cols[part][-1] + 1) * T)
        for c in range(CHUNKS):
            if part == 0:
                rows = pl.ds(c * per, per)
                pltpu.make_async_copy(d_hbm.at[rows], d_v.at[rows], d_sem.at[c]).wait()
            for f in range(c * per, (c + 1) * per):
                left = jnp.concatenate([d_v[f, k] for k in range(D)], axis=1)
                right = jnp.concatenate([pm[dcols[k, f], :, at] for k in range(D)], axis=0)
                x[f * T : (f + 1) * T, at] = jnp.dot(
                    left, right, preferred_element_type=f32
                ).astype(bf16)
                if part == 0:
                    pmt[:, f * T : (f + 1) * T] = pm[f].T
            if part == 0 and c == CHUNKS - 2:
                enter()
        loc[:, at] = jnp.dot(pmt[T:, :], x[:, at], preferred_element_type=f32)

    def stage(b, part):
        for s, b2 in sent[b].items():
            if b2 in cols[part]:
                gs[b - 1, s] = loc[(b - 1) * T : b * T, b2 * T : (b2 + 1) * T].astype(bf16)

    def stage_rest(b):
        for s in range(base, CT):
            gs[b - 1, s] = tt[spot(b, s), b * T : (b + 1) * T, :].astype(bf16)

    ids = [lax.rem(m + moff[i], M) * S + s for i in range(3) for s in range(S)]
    zero = jnp.zeros((T, T), bf16)

    def remote_mid(lo, hi):
        return jnp.dot(pmt[lo:hi, :], ar[...], preferred_element_type=f32).astype(bf16)

    def remote(mid, lo, hi, arrive):
        for i in range(3):
            if arrive:
                m_copies[back[i]].wait_recv()
            res = None
            for s in range(S):
                r = i * S + s
                term = jnp.dot(
                    mid[:, r * T : (r + 1) * T], rbuf[i, s], preferred_element_type=f32
                )
                res = term if res is None else res + term
            for b2 in range(B):
                tt[i * B + b2, lo:hi] = res[:, b2 * T : (b2 + 1) * T]

    cand = [
        lax.rem(g + hoff[b2], G) * M + lax.rem(m + moff[i], M)
        for i in range(3)
        for b2 in range(B)
    ]

    def spot(b, s):
        col = ccols[s, own[b]]
        at = jnp.int32(3 * B)
        for n, c in enumerate(cand):
            at = jnp.where(col == c, n, at)
        return at

    local_part(0)
    for b in (1, 2):
        stage(b, 0)
        start(b, spans[b][0])

    o_copy.wait()
    for f in range(R):
        for r, ident in enumerate(ids):
            block = None
            for k in range(O):
                live = jnp.logical_and(ocols[k, f] == ident, ocount[f] > k)
                term = jnp.where(live, o_v[f, k], zero)
                block = term if block is None else block + term
            ar[f * T : (f + 1) * T, r * T : (r + 1) * T] = block
    mid = remote_mid(T, B * T)

    tt[3 * B] = jnp.zeros(tt.shape[1:], f32)
    remote(mid, T, B * T, True)
    stage_rest(1)
    stage_rest(2)
    start_feeds()
    local_part(1)
    for b in (1, 2):
        stage(b, 1)
        start(b, spans[b][1])
    for b in (1, 2):
        start_rest(b)

    local = jnp.dot(pmt[:T, :], x[...], preferred_element_type=f32)
    for s in range(base):
        if s in sent[0]:
            b2 = sent[0][s]
            kept_v[s] = local[:, b2 * T : (b2 + 1) * T]
        else:
            kept_v[s] = jnp.zeros((T, T), f32)
    relay()
    remote(remote_mid(0, T), 0, T, False)
    for s in range(base, CT):
        kept_v[s] = tt[spot(0, s), :T, :]
    keep = pltpu.make_async_copy(kept_v, kept, k_sem)
    keep.start()

    each_fill(lambda copy: copy.wait())
    keep.wait()
    for copy in m_copies:
        copy.wait_send()
    for b in range(1, B):
        for which in spans[b] + [rest]:
            each_send(b, which, lambda copy: copy.wait_send())
        for lo, n in spans[b][0] + spans[b][1]:
            group_copy(b, lo, n).wait_recv()

        def last(b=b):
            for lo, n in rest:
                group_copy(b, lo, n).wait_recv()

        if not relays:
            last()
            continue

        @pl.when(g == relays[b])
        def _(b=b):
            for lo, n in rest:
                group_copy(b, lo, n).wait_send()

        to = (relays[b] + hoff[b]) % G
        pl.when(jnp.logical_or(g == to, lax.rem(g, 2) == 1))(last)


def on_device(
    G,
    M,
    diag_tiles,
    diag_cols,
    offd_tiles,
    offd_cols,
    offd_count,
    p_tiles,
    p_cols,
    send_rows,
    coarse_cols,
):
    R, PT, T, _ = p_tiles.shape
    D, O = diag_tiles.shape[1], offd_tiles.shape[1]
    S = send_rows.shape[2]
    CT = coarse_cols.shape[1]
    B = 3
    bf16, f32 = jnp.bfloat16, jnp.float32
    i32 = jnp.int32
    hbm = pl.BlockSpec(memory_space=pl.ANY)
    kept, got = pl.pallas_call(
        functools.partial(kernel, G, M),
        out_shape=(
            jax.ShapeDtypeStruct((CT, T, T), f32),
            jax.ShapeDtypeStruct((B - 1, CT, T, T), bf16),
        ),
        in_specs=[hbm] * 9,
        out_specs=(hbm, hbm),
        scratch_shapes=[
            pltpu.VMEM((R, PT, T, T), bf16),
            pltpu.VMEM((R, D, T, T), bf16),
            pltpu.VMEM((R, O, T, T), bf16),
            pltpu.VMEM((R, T, B * T), bf16),
            pltpu.VMEM((B * T, R * T), bf16),
            pltpu.VMEM((R * T, B * T), bf16),
            pltpu.VMEM((R * T, 3 * S * T), bf16),
            pltpu.VMEM((3, S, T, B * T), bf16),
            pltpu.VMEM((3, S, T, B * T), bf16),
            pltpu.VMEM((CT, T, T), bf16),
            pltpu.VMEM((CT, T, T), f32),
            pltpu.VMEM((3 * B + 1, B * T, T), f32),
            pltpu.VMEM((B - 1, CT, T, T), bf16),
            pltpu.VMEM(((B - 1) * T, B * T), f32),
            pltpu.VMEM((CT, T, T), bf16),
            pltpu.SMEM((D, R), i32),
            pltpu.SMEM((O, R), i32),
            pltpu.SMEM((R,), i32),
            pltpu.SMEM((PT, R), i32),
            pltpu.SMEM((1, S, send_rows.shape[1]), i32),
            pltpu.SMEM((CT, coarse_cols.shape[0]), i32),
            pltpu.SemaphoreType.DMA((6,)),
            pltpu.SemaphoreType.DMA((CHUNKS,)),
            pltpu.SemaphoreType.DMA((CHUNKS,)),
            pltpu.SemaphoreType.DMA,
            pltpu.SemaphoreType.DMA((3,)),
            pltpu.SemaphoreType.DMA((3,)),
            pltpu.SemaphoreType.DMA((B - 1, CT)),
            pltpu.SemaphoreType.DMA((B - 1, CT)),
            pltpu.SemaphoreType.DMA((B - 1, CT)),
            pltpu.SemaphoreType.DMA,
            pltpu.SemaphoreType.DMA((CT,)),
        ],
        compiler_params=pltpu.CompilerParams(
            collective_id=0, has_side_effects=True, vmem_limit_bytes=63 * 1024 * 1024
        ),
    )(
        diag_cols.T,
        offd_cols.T,
        offd_count,
        p_cols.T,
        jnp.swapaxes(send_rows, 1, 2),
        coarse_cols.T,
        p_tiles,
        diag_tiles,
        offd_tiles,
    )
    return (kept + got[0].astype(f32) + got[1].astype(f32))[None]


def solution(mesh):
    return jax.shard_map(
        functools.partial(on_device, mesh.shape["group"], mesh.shape["member"]),
        mesh=mesh,
        in_specs=(
            P(("group", "member"), None, None, None),
            P(("group", "member"), None),
            P(("group", "member"), None, None, None),
            P(("group", "member"), None),
            P(("group", "member")),
            P(("group", "member"), None, None, None),
            P(("group", "member"), None),
            P(("group", "member"), None, None),
            P(),
        ),
        out_specs=P(("group", "member"), None, None, None),
        check_vma=False,
    )
```

```python
import functools

import jax
import jax.numpy as jnp
from jax import lax
from jax.experimental import pallas as pl
from jax.experimental.pallas import tpu as pltpu
from jax.sharding import PartitionSpec as P

MESH = pl.DeviceIdType.MESH
CHUNKS = 4


def kernel(
    G,
    M,
    dcols_hbm,
    ocols_hbm,
    ocount_hbm,
    pcols_hbm,
    srows_hbm,
    ccols_hbm,
    p_hbm,
    d_hbm,
    o_hbm,
    kept,
    got,
    p_v,
    d_v,
    o_v,
    pm,
    pmt,
    x,
    ar,
    sbuf,
    rbuf,
    zeros,
    kept_v,
    tt,
    gs,
    loc,
    fed_v,
    dcols,
    ocols,
    ocount,
    pcols,
    srows,
    ccols,
    i_sem,
    p_sem,
    d_sem,
    o_sem,
    ms_sem,
    mr_sem,
    gs_sem,
    gr_sem,
    z_sem,
    k_sem,
    f_sem,
):
    R, PT, T = p_v.shape[0], p_v.shape[1], p_v.shape[2]
    D, O = d_v.shape[1], o_v.shape[1]
    S = srows.shape[1]
    CT = ccols.shape[0]
    per = R // CHUNKS
    hoff = (0, 1, G // 2)
    moff = (M - 1, 1, M // 2)
    back = (1, 0, 2)
    coff = (0, 1, G - 1, G // 2)
    B = len(hoff)
    g = lax.axis_index("group")
    m = lax.axis_index("member")
    f32, bf16 = jnp.float32, jnp.bfloat16

    ints = ((pcols_hbm, pcols), (srows_hbm, srows), (dcols_hbm, dcols))
    ints += ((ocols_hbm, ocols), (ocount_hbm, ocount), (ccols_hbm, ccols))
    i_copies = [pltpu.make_async_copy(a, b, i_sem.at[n]) for n, (a, b) in enumerate(ints)]
    for copy in i_copies:
        copy.start()
    o_copy = pltpu.make_async_copy(o_hbm, o_v, o_sem)
    p_copies = []
    for c in range(CHUNKS):
        rows = pl.ds(c * per, per)
        p_copies.append(pltpu.make_async_copy(p_hbm.at[rows], p_v.at[rows], p_sem.at[c]))
        p_copies[-1].start()
    for c in range(CHUNKS):
        rows = pl.ds(c * per, per)
        pltpu.make_async_copy(d_hbm.at[rows], d_v.at[rows], d_sem.at[c]).start()
    o_copy.start()

    barrier = pltpu.get_barrier_semaphore()
    peers = [(g, lax.rem(m + d, M)) for d in moff]
    peers += [(lax.rem(g + d, G), m) for d in (1, G - 1, G // 2)]
    for peer in peers:
        pl.semaphore_signal(barrier, inc=1, device_id=peer, device_id_type=MESH)

    own = [lax.rem(g + d, G) * M + m for d in hoff]
    base = len(coff)

    sent = []
    for b in range(B):
        rel = [(hoff[b] + d) % G for d in coff]
        sent.append({s: hoff.index(r) for s, r in enumerate(rel) if r in hoff})
    relays = {1: 1, 2: 2} if G == 4 else {}
    feeds = {1: 3, 2: 0} if G == 4 else {}

    def runs(have):
        found = []
        for s in sorted(have):
            if found and sum(found[-1]) == s:
                found[-1] = (found[-1][0], found[-1][1] + 1)
            else:
                found.append((s, 1))
        return found

    def fill(b, lo, n):
        where = pl.ds(lo, n)
        return pltpu.make_async_copy(zeros.at[pl.ds(0, n)], got.at[b - 1, where], z_sem.at[b - 1, lo])

    def each_fill(act):
        for b in range(1, B):
            gap = runs(set(range(base)) - set(sent[b]))

            def some(b=b, gap=gap):
                for lo, n in gap:
                    act(fill(b, lo, n))

            some()
            if not relays:
                continue
            other = B - b

            @pl.when(g == (relays[b] + hoff[b]) % G)
            def _(other=other):
                act(fill(other, base, CT - base))

    zeros[...] = jnp.zeros((CT, T, T), bf16)
    each_fill(lambda copy: copy.start())

    for copy in i_copies:
        copy.wait()
    for f in range(R):
        if f % per == 0:
            p_copies[f // per].wait()
        parts = []
        for b in range(B):
            block = jnp.zeros((T, T), bf16)
            for q in range(PT):
                block = jnp.where(pcols[q, f] == own[b], p_v[f, q], block)
            parts.append(block)
        pm[f] = jnp.concatenate(parts, axis=1)

    for i in range(3):
        to = lax.rem(m + moff[i], M)
        for s in range(S):
            sbuf[i, s] = pm[srows[0, s, to]]

    m_copies = [
        pltpu.make_async_remote_copy(
            src_ref=sbuf.at[i],
            dst_ref=rbuf.at[back[i]],
            send_sem=ms_sem.at[i],
            recv_sem=mr_sem.at[back[i]],
            device_id=(g, lax.rem(m + moff[i], M)),
            device_id_type=MESH,
        )
        for i in range(3)
    ]

    def enter():
        pl.semaphore_wait(barrier, len(peers))
        for copy in m_copies:
            copy.start()

    def group_copy(b, lo, n):
        where = pl.ds(lo, n)
        return pltpu.make_async_remote_copy(
            src_ref=gs.at[b - 1, where],
            dst_ref=got.at[b - 1, where],
            send_sem=gs_sem.at[b - 1, lo],
            recv_sem=gr_sem.at[b - 1, lo],
            device_id=(lax.rem(g + hoff[b], G), m),
            device_id_type=MESH,
        )

    def feed_copy(b, lo, n):
        where = pl.ds(lo, n)
        return pltpu.make_async_remote_copy(
            src_ref=gs.at[b - 1, where],
            dst_ref=fed_v.at[where],
            send_sem=gs_sem.at[b - 1, lo],
            recv_sem=f_sem.at[lo],
            device_id=(relays[B - b], m),
            device_id_type=MESH,
        )

    cols = ((0, 1), (2,))
    spans = {
        b: [runs(s for s, b2 in sent[b].items() if b2 in part) for part in cols]
        for b in range(1, B)
    }
    rest = [(s, 1) for s in range(base, CT)]

    def each_send(b, which, act):
        def direct():
            for lo, n in which:
                act(group_copy(b, lo, n))

        if not relays or which is not rest:
            direct()
            return
        pl.when(jnp.logical_and(g != feeds[b], g != relays[b]))(direct)

        @pl.when(g == feeds[b])
        def _():
            for lo, n in which:
                act(feed_copy(b, lo, n))

    def start(b, which):
        each_send(b, which, lambda copy: copy.start())

    def start_feeds():
        for b in relays:

            @pl.when(g == feeds[b])
            def _(b=b):
                for lo, n in rest:
                    feed_copy(b, lo, n).start()

    def start_rest(b):
        def direct():
            for lo, n in rest:
                group_copy(b, lo, n).start()

        if relays:
            pl.when(jnp.logical_and(g != feeds[b], g != relays[b]))(direct)
        else:
            direct()

    def add_and_send(b, lo, n):
        feed_copy(B - b, lo, n).wait_recv()
        for s in range(lo, lo + n):
            total = tt[spot(b, s), b * T : (b + 1) * T, :] + fed_v[s].astype(f32)
            gs[b - 1, s] = total.astype(bf16)
        group_copy(b, lo, n).start()

    def relay():
        for b in relays:

            @pl.when(g == relays[b])
            def _(b=b):
                for lo, n in rest:
                    add_and_send(b, lo, n)

    def local_part(part):
        at = slice(cols[part][0] * T, (cols[part][-1] + 1) * T)
        for c in range(CHUNKS):
            if part == 0:
                rows = pl.ds(c * per, per)
                pltpu.make_async_copy(d_hbm.at[rows], d_v.at[rows], d_sem.at[c]).wait()
            for f in range(c * per, (c + 1) * per):
                left = jnp.concatenate([d_v[f, k] for k in range(D)], axis=1)
                right = jnp.concatenate([pm[dcols[k, f], :, at] for k in range(D)], axis=0)
                x[f * T : (f + 1) * T, at] = jnp.dot(
                    left, right, preferred_element_type=f32
                ).astype(bf16)
                if part == 0:
                    pmt[:, f * T : (f + 1) * T] = pm[f].T
            if part == 0 and c == CHUNKS - 2:
                enter()
        loc[:, at] = jnp.dot(pmt[T:, :], x[:, at], preferred_element_type=f32)

    def stage(b, part):
        for s, b2 in sent[b].items():
            if b2 in cols[part]:
                gs[b - 1, s] = loc[(b - 1) * T : b * T, b2 * T : (b2 + 1) * T].astype(bf16)

    def stage_rest(b):
        for s in range(base, CT):
            gs[b - 1, s] = tt[spot(b, s), b * T : (b + 1) * T, :].astype(bf16)

    ids = [lax.rem(m + moff[i], M) * S + s for i in range(3) for s in range(S)]
    zero = jnp.zeros((T, T), bf16)

    def remote_mid(lo, hi):
        return jnp.dot(pmt[lo:hi, :], ar[...], preferred_element_type=f32).astype(bf16)

    def remote(mid, lo, hi, arrive):
        for i in range(3):
            if arrive:
                m_copies[back[i]].wait_recv()
            res = None
            for s in range(S):
                r = i * S + s
                term = jnp.dot(
                    mid[:, r * T : (r + 1) * T], rbuf[i, s], preferred_element_type=f32
                )
                res = term if res is None else res + term
            for b2 in range(B):
                tt[i * B + b2, lo:hi] = res[:, b2 * T : (b2 + 1) * T]

    cand = [
        lax.rem(g + hoff[b2], G) * M + lax.rem(m + moff[i], M)
        for i in range(3)
        for b2 in range(B)
    ]

    def spot(b, s):
        col = ccols[s, own[b]]
        at = jnp.int32(3 * B)
        for n, c in enumerate(cand):
            at = jnp.where(col == c, n, at)
        return at

    local_part(0)
    for b in (1, 2):
        stage(b, 0)
        start(b, spans[b][0])

    o_copy.wait()
    for f in range(R):
        for r, ident in enumerate(ids):
            block = None
            for k in range(O):
                live = jnp.logical_and(ocols[k, f] == ident, ocount[f] > k)
                term = jnp.where(live, o_v[f, k], zero)
                block = term if block is None else block + term
            ar[f * T : (f + 1) * T, r * T : (r + 1) * T] = block
    mid = remote_mid(T, B * T)

    tt[3 * B] = jnp.zeros(tt.shape[1:], f32)
    remote(mid, T, B * T, True)
    stage_rest(1)
    stage_rest(2)
    start_feeds()
    local_part(1)
    for b in (1, 2):
        stage(b, 1)
        start(b, spans[b][1])
    for b in (1, 2):
        start_rest(b)

    relay()

    local = jnp.dot(pmt[:T, :], x[...], preferred_element_type=f32)
    for s in range(base):
        if s in sent[0]:
            b2 = sent[0][s]
            kept_v[s] = local[:, b2 * T : (b2 + 1) * T]
        else:
            kept_v[s] = jnp.zeros((T, T), f32)
    remote(remote_mid(0, T), 0, T, False)
    for s in range(base, CT):
        kept_v[s] = tt[spot(0, s), :T, :]
    keep = pltpu.make_async_copy(kept_v, kept, k_sem)
    keep.start()

    each_fill(lambda copy: copy.wait())
    keep.wait()
    for copy in m_copies:
        copy.wait_send()
    for b in range(1, B):
        for which in spans[b] + [rest]:
            each_send(b, which, lambda copy: copy.wait_send())
        for lo, n in spans[b][0] + spans[b][1]:
            group_copy(b, lo, n).wait_recv()

        def last(b=b):
            for lo, n in rest:
                group_copy(b, lo, n).wait_recv()

        if not relays:
            last()
            continue

        @pl.when(g == relays[b])
        def _(b=b):
            for lo, n in rest:
                group_copy(b, lo, n).wait_send()

        to = (relays[b] + hoff[b]) % G
        pl.when(jnp.logical_or(g == to, lax.rem(g, 2) == 1))(last)


def on_device(
    G,
    M,
    diag_tiles,
    diag_cols,
    offd_tiles,
    offd_cols,
    offd_count,
    p_tiles,
    p_cols,
    send_rows,
    coarse_cols,
):
    R, PT, T, _ = p_tiles.shape
    D, O = diag_tiles.shape[1], offd_tiles.shape[1]
    S = send_rows.shape[2]
    CT = coarse_cols.shape[1]
    B = 3
    bf16, f32 = jnp.bfloat16, jnp.float32
    i32 = jnp.int32
    hbm = pl.BlockSpec(memory_space=pl.ANY)
    kept, got = pl.pallas_call(
        functools.partial(kernel, G, M),
        out_shape=(
            jax.ShapeDtypeStruct((CT, T, T), f32),
            jax.ShapeDtypeStruct((B - 1, CT, T, T), bf16),
        ),
        in_specs=[hbm] * 9,
        out_specs=(hbm, hbm),
        scratch_shapes=[
            pltpu.VMEM((R, PT, T, T), bf16),
            pltpu.VMEM((R, D, T, T), bf16),
            pltpu.VMEM((R, O, T, T), bf16),
            pltpu.VMEM((R, T, B * T), bf16),
            pltpu.VMEM((B * T, R * T), bf16),
            pltpu.VMEM((R * T, B * T), bf16),
            pltpu.VMEM((R * T, 3 * S * T), bf16),
            pltpu.VMEM((3, S, T, B * T), bf16),
            pltpu.VMEM((3, S, T, B * T), bf16),
            pltpu.VMEM((CT, T, T), bf16),
            pltpu.VMEM((CT, T, T), f32),
            pltpu.VMEM((3 * B + 1, B * T, T), f32),
            pltpu.VMEM((B - 1, CT, T, T), bf16),
            pltpu.VMEM(((B - 1) * T, B * T), f32),
            pltpu.VMEM((CT, T, T), bf16),
            pltpu.SMEM((D, R), i32),
            pltpu.SMEM((O, R), i32),
            pltpu.SMEM((R,), i32),
            pltpu.SMEM((PT, R), i32),
            pltpu.SMEM((1, S, send_rows.shape[1]), i32),
            pltpu.SMEM((CT, coarse_cols.shape[0]), i32),
            pltpu.SemaphoreType.DMA((6,)),
            pltpu.SemaphoreType.DMA((CHUNKS,)),
            pltpu.SemaphoreType.DMA((CHUNKS,)),
            pltpu.SemaphoreType.DMA,
            pltpu.SemaphoreType.DMA((3,)),
            pltpu.SemaphoreType.DMA((3,)),
            pltpu.SemaphoreType.DMA((B - 1, CT)),
            pltpu.SemaphoreType.DMA((B - 1, CT)),
            pltpu.SemaphoreType.DMA((B - 1, CT)),
            pltpu.SemaphoreType.DMA,
            pltpu.SemaphoreType.DMA((CT,)),
        ],
        compiler_params=pltpu.CompilerParams(
            collective_id=0, has_side_effects=True, vmem_limit_bytes=63 * 1024 * 1024
        ),
    )(
        diag_cols.T,
        offd_cols.T,
        offd_count,
        p_cols.T,
        jnp.swapaxes(send_rows, 1, 2),
        coarse_cols.T,
        p_tiles,
        diag_tiles,
        offd_tiles,
    )
    return (kept + got[0].astype(f32) + got[1].astype(f32))[None]


def solution(mesh):
    return jax.shard_map(
        functools.partial(on_device, mesh.shape["group"], mesh.shape["member"]),
        mesh=mesh,
        in_specs=(
            P(("group", "member"), None, None, None),
            P(("group", "member"), None),
            P(("group", "member"), None, None, None),
            P(("group", "member"), None),
            P(("group", "member")),
            P(("group", "member"), None, None, None),
            P(("group", "member"), None),
            P(("group", "member"), None, None),
            P(),
        ),
        out_specs=P(("group", "member"), None, None, None),
        check_vma=False,
    )
```
